512 devices in a mesh: dp: 4 (over x_hi, core), lat: 16 (over y, x_lo), lon: 8 (over z).
Axes of the slice: x: 4 (x_hi: 2, x_lo: 2; x = x_hi * 2 + x_lo), y: 8, z: 8, core: 2. Of those that a mesh axis runs over, the one named last changes fastest.
Arguments:
- state: bfloat16 [4, 32, 1440, 384], P('dp', 'lat', 'lon'), may hold values from -6 to 6
- cotangent: bfloat16 [4, 32, 1440, 384], P('dp', 'lat', 'lon'), may hold values from -6 to 6
- weights: bfloat16 [4, 384, 384], replicated, may hold values from -0.15625 to 0.15625
- lat_off: int32 [32, 16], replicated, may hold values from -2 to 2
- lon_off: int32 [32, 16], replicated, may hold values from -24 to 24
- basis: int32 [32, 16], replicated, may hold values from 0 to 3
- tap_val: float32 [32, 16], replicated, may hold values from -1.5 to 1.5
- tap_count: int32 [32], replicated, may hold values from 2 to 16
Outputs:
- new_state: bfloat16 [4, 32, 1440, 384], P('dp', 'lat', 'lon')
- state_grad: bfloat16 [4, 32, 1440, 384], P('dp', 'lat', 'lon')
- weight_grad: bfloat16 [4, 384, 384], replicated
The draws below stay inside these ranges and needn't reach their ends.
All inputs are finite; a program needn't handle non-finite values.
Results may differ from the reference program's by a relative error of at most 0.0048.
The reference program's roundings to bfloat16 on the way count: a program that leaves them out, or rounds other values in their place, can miss the bound.
Values may be sent and summed in bfloat16 or wider, within the bound.
No kernel may reach another device: no remote copies, remote signals or barrier semaphores. Data moves between devices by JAX's collectives and lax.ppermute only.
A program may use at most 64 MiB of HBM per device.

```python
import jax
import jax.numpy as jnp
from jax import lax

C = 384
LON = 1440
KBASIS = 4
TAPS = 16
H = 2
LONREACH = 24
LATB = 32
SAMPLES = 4
CELLS = 184320


def draw_lat_off(key, part):
    key = jax.random.fold_in(key, 11)
    values = jax.random.randint(key, (LATB, TAPS), -H, H + 1)
    values = values.at[:, 0].set(-H).at[:, 1].set(H)
    return values.astype(jnp.int32)


def draw_lon_off(key, part):
    key = jax.random.fold_in(key, 12)
    row_ids = jnp.arange(LATB, dtype=jnp.int32)
    spread = 1 + (LONREACH - 1) * row_ids // max(LATB - 1, 1)
    values = jax.random.randint(key, (LATB, TAPS), -spread[:, None], spread[:, None] + 1)
    values = values.at[LATB - 1, 0].set(LONREACH).at[LATB - 1, 1].set(-LONREACH)
    return values.astype(jnp.int32)


def draw_tap_count(key, part):
    key = jax.random.fold_in(key, 13)
    row_ids = jnp.arange(LATB, dtype=jnp.int32)
    base = TAPS // 4 + (TAPS - TAPS // 4) * row_ids // max(LATB - 1, 1)
    jitter = jax.random.randint(key, (LATB,), 0, 3)
    values = jnp.clip(base - jitter, 2, TAPS)
    values = values.at[LATB - 1].set(TAPS)
    return values.astype(jnp.int32)


def place_ends(values, own_key, smallest, high):
    extent = values.shape
    index_at = [jax.random.randint(jax.random.fold_in(own_key, axis), (), 0, extent[axis]) for axis in range(len(extent))]
    values = values.at[tuple(index_at)].set(smallest)
    longest = extent.index(max(extent))
    index_at[longest] = (index_at[longest] + 1) % extent[longest]
    return values.at[tuple(index_at)].set(high)


def block_scale(own_key, extent, split, low, high):
    factor_of, own = 1.0, jax.random.fold_in(own_key, 6)
    for axis_at, shards_of in split:
        draws = jnp.exp(jax.random.uniform(jax.random.fold_in(own, axis_at), (shards_of,), jnp.float32, low / len(split), high / len(split)))
        factor_of = factor_of * jnp.repeat(draws, extent[axis_at] // shards_of).reshape([-1 if axis == axis_at else 1 for axis in range(len(extent))])
    return factor_of


def scatter_about(key, extent, scale, bound, split=(), kind=jnp.bfloat16):
    array = jax.random.normal(key, extent, jnp.float32) * scale
    if len(split) > 0:
        array = block_scale(key, extent, split, -0.22, 0.18) * array
    return jnp.clip(array, min=-bound, max=bound).astype(kind)


def setup_inputs(seed: int = 0) -> dict:
    arg_keys = jax.random.split(jax.random.key(seed), 9)
    state = scatter_about(arg_keys[0], (SAMPLES, LATB, LON, C), 1.0, 6.0, ((0, 4), (1, 16), (2, 8)))
    cotangent = scatter_about(arg_keys[1], (SAMPLES, LATB, LON, C), 1.0, 6.0, ((0, 4), (1, 16), (2, 8)))
    weights = scatter_about(arg_keys[2], (KBASIS, C, C), (KBASIS * C) ** -0.5, 0.15625)
    lat_off = draw_lat_off(jax.random.fold_in(arg_keys[8], 71), 0)
    lon_off = draw_lon_off(jax.random.fold_in(arg_keys[8], 71), 0)
    basis = place_ends(jax.random.randint(arg_keys[5], (LATB, TAPS), 0, KBASIS), jax.random.fold_in(arg_keys[5], 1), 0, KBASIS - 1).astype(jnp.int32)
    tap_val = scatter_about(arg_keys[6], (LATB, TAPS), 0.3, 1.5, (), jnp.float32)
    tap_count = draw_tap_count(jax.random.fold_in(arg_keys[8], 71), 0)
    return dict(state=state, cotangent=cotangent, weights=weights, lat_off=lat_off, lon_off=lon_off, basis=basis, tap_val=tap_val, tap_count=tap_count)


def basis_conv(field, lat_off, lon_off, basis, tap_val, tap_count):
    padded = jnp.pad(field, ((H, H), (0, 0), (0, 0)))
    row_ids = jnp.arange(LATB, dtype=jnp.int32)
    col_ids = jnp.arange(LON, dtype=jnp.int32)

    def add_tap(total, tap_index):
        lat_step = lat_off[:, tap_index]
        lon_step = lon_off[:, tap_index]
        kind = basis[:, tap_index]
        weight = jnp.where(tap_index < tap_count, tap_val[:, tap_index], 0.0)
        source_rows = row_ids + H + lat_step
        source_cols = (col_ids[None, :] + lon_step[:, None]) % LON
        piece = padded[source_rows[:, None], source_cols]
        return (total.at[kind, row_ids].add(weight[:, None, None] * piece), None)
    start = jnp.zeros((KBASIS, LATB, LON, C), dtype=jnp.float32)
    total, _ = lax.scan(add_tap, start, jnp.arange(TAPS, dtype=jnp.int32))
    return total

def reference(state, cotangent, weights, lat_off, lon_off, basis, tap_val, tap_count):
    weights_wide = weights.astype(jnp.float32)

    def conv(field):
        return basis_conv(field, lat_off, lon_off, basis, tap_val, tap_count)

    def one_sample(pair):
        field, upstream = pair
        z_basis = conv(field.astype(jnp.float32)).astype(jnp.bfloat16)
        mixed = jnp.einsum('krjc,kcd->rjd', z_basis.astype(jnp.float32), weights_wide)
        activated, gelu_back = jax.vjp(jax.nn.gelu, mixed)
        new_field = (field.astype(jnp.float32) + activated).astype(jnp.bfloat16)
        dmixed = gelu_back(upstream.astype(jnp.float32))[0].astype(jnp.bfloat16)
        part_grad = jnp.einsum('krjc,rjd->kcd', z_basis.astype(jnp.float32), dmixed.astype(jnp.float32))
        dz_basis = jnp.einsum('rjd,kcd->krjc', dmixed.astype(jnp.float32), weights_wide).astype(jnp.bfloat16)
        _, conv_back = jax.vjp(conv, field.astype(jnp.float32))
        adjoint = conv_back(dz_basis.astype(jnp.float32))[0].astype(jnp.bfloat16)
        field_grad = (upstream.astype(jnp.float32) + adjoint.astype(jnp.float32)).astype(jnp.bfloat16)
        return (new_field, field_grad, part_grad)
    new_state, state_grad, part_grads = lax.map(one_sample, (state, cotangent))
    weight_grad = (lax.optimization_barrier(jnp.sum(part_grads, axis=0)) / jnp.sqrt(jnp.float32(CELLS))).astype(jnp.bfloat16)
    return (new_state, state_grad, weight_grad)
```

```python
import functools
import math

import jax
import jax.numpy as jnp
from jax import lax
from jax.experimental import pallas as pl
from jax.experimental.pallas import tpu as pltpu
from jax.sharding import PartitionSpec as P

H = 2
LONREACH = 24
LANES = 128
ROW = 192
EXT = ROW + 2 * LONREACH
SLOPE = math.sqrt(2.0 / math.pi)
CUBIC = 0.044715

SMEM = pl.BlockSpec(memory_space=pltpu.SMEM)
VMEM = pl.BlockSpec(memory_space=pltpu.VMEM)


def plan_kernel(lat_off, lon_off, basis, tap_val, tap_count, f_pos, f_val, f_seg, b_pos, b_val, b_num):
    rows, kcount = f_seg.shape[0] // 8, 4
    taps = lat_off.shape[1]
    total = lat_off.shape[0]
    first = lax.axis_index("lat") * rows
    for i in range(rows):
        row = first + i
        used = tap_count[row]
        slot = jnp.int32(0)
        for k in range(kcount):
            f_seg[i * 8 + k] = slot

            def add(t, slot):
                hit = basis[row, t] == k

                @pl.when(hit)
                def _():
                    f_pos[i * taps + slot] = (i + H + lat_off[row, t]) * EXT + LONREACH + lon_off[row, t]
                    f_val[i * taps + slot] = tap_val[row, t]

                return slot + hit.astype(jnp.int32)

            slot = lax.fori_loop(0, used, add, slot)
        f_seg[i * 8 + kcount] = slot
    room = b_pos.shape[0] // rows
    counts = tuple(jnp.int32(0) for _ in range(rows))
    for e in range(rows + 2 * H):
        row = first + (e - H)
        inside = (row >= 0) & (row < total)
        row = jnp.clip(row, 0, total - 1)
        used = jnp.where(inside, tap_count[row], 0)

        def give(t, counts):
            target = e - H + lat_off[row, t]
            new = []
            for i in range(rows):
                hit = target == i

                @pl.when(hit)
                def _():
                    at = i * room + counts[i]
                    b_pos[at] = (basis[row, t] * (rows + 2 * H) + e) * EXT + LONREACH - lon_off[row, t]
                    b_val[at] = tap_val[row, t]

                new.append(counts[i] + hit.astype(jnp.int32))
            return tuple(new)

        counts = lax.fori_loop(0, used, give, counts)
    for i in range(rows):
        b_num[i] = counts[i]


def plan(tables, rows):
    taps = tables[0].shape[1]
    room = (rows + 2 * H) * taps
    shapes = [
        jax.ShapeDtypeStruct((rows * taps,), jnp.int32),
        jax.ShapeDtypeStruct((rows * taps,), jnp.float32),
        jax.ShapeDtypeStruct((rows * 8,), jnp.int32),
        jax.ShapeDtypeStruct((rows * room,), jnp.int32),
        jax.ShapeDtypeStruct((rows * room,), jnp.float32),
        jax.ShapeDtypeStruct((8,), jnp.int32),
    ]
    return pl.pallas_call(
        plan_kernel,
        out_shape=shapes,
        in_specs=[SMEM] * 5,
        out_specs=[SMEM] * 6,
    )(*tables)


def pieces(own, north, south, west, east, nw, ne, sw, se):
    rows = own.shape[0]
    out = []
    for side, w, mid, e in ((0, nw, north, ne), (rows, west, own, east), (2 * rows, sw, south, se)):
        for r in range(rows):
            out.append((side + r, w, mid, e, r))
    return out


def forward_kernel(f_pos, f_val, f_seg, own, north, south, west, east, nw, ne, sw, se, upstream, weights,
                   new_state, dmixed, d_west, d_east, grad, ext, z, dm):
    rows, width, channels = own.shape
    kcount = weights.shape[0] // channels
    taps = f_pos.shape[0] // rows
    chunks = channels // LANES
    for q, w, mid, e, r in pieces(own, north, south, west, east, nw, ne, sw, se):
        base = q * EXT
        for c in range(chunks):
            lanes = slice(c * LANES, (c + 1) * LANES)
            ext[c, base + LONREACH + width : base + EXT, :] = jnp.zeros((EXT - LONREACH - width, LANES), jnp.float32)
            ext[c, base : base + LONREACH, :] = w[r, :, lanes].astype(jnp.float32)
            ext[c, base + LONREACH : base + LONREACH + width, :] = mid[r, :, lanes].astype(jnp.float32)
            ext[c, base + LONREACH + width : base + 2 * LONREACH + width, :] = e[r, :, lanes].astype(jnp.float32)
    for i in range(rows):
        for k in range(kcount):
            for c in range(chunks):

                def add(n, acc):
                    at = i * taps + n
                    return acc + f_val[at] * ext[c, pl.ds(f_pos[at], ROW), :]

                acc = lax.fori_loop(
                    f_seg[i * 8 + k], f_seg[i * 8 + k + 1], add, jnp.zeros((ROW, LANES), jnp.float32)
                )
                col = k * channels + c * LANES
                z[i * ROW : (i + 1) * ROW, col : col + LANES] = acc.astype(jnp.bfloat16)
    mixed = jnp.dot(z[...], weights[...], preferred_element_type=jnp.float32)
    for i in range(rows):
        x = mixed[i * ROW : i * ROW + width]
        square = x * x
        t = jnp.tanh(SLOPE * (x + CUBIC * (square * x)))
        cdf = 0.5 * (1.0 + t)
        new_state[i] = (own[i].astype(jnp.float32) + x * cdf).astype(jnp.bfloat16)
        slope = cdf + x * (0.5 * (1.0 - t * t)) * (SLOPE * (1.0 + (3.0 * CUBIC) * square))
        d = (upstream[i].astype(jnp.float32) * slope).astype(jnp.bfloat16)
        dmixed[i] = d
        d_west[i] = d[:LONREACH]
        d_east[i] = d[width - LONREACH :]
        dm[i * ROW : (i + 1) * ROW, :] = jnp.concatenate(
            [d, jnp.zeros((ROW - width, channels), jnp.bfloat16)], axis=0
        )
    grad[...] = lax.dot_general(
        z[...], dm[...], (((0,), (0,)), ((), ())), preferred_element_type=jnp.float32
    )


def forward(lists, around, upstream, weights):
    rows, width, channels = upstream.shape
    wide = weights.shape[0]
    block = jax.ShapeDtypeStruct((rows, width, channels), jnp.bfloat16)
    rim = jax.ShapeDtypeStruct((rows, LONREACH, channels), jnp.bfloat16)
    return pl.pallas_call(
        forward_kernel,
        out_shape=[block, block, rim, rim, jax.ShapeDtypeStruct((wide, channels), jnp.float32)],
        in_specs=[SMEM] * 3 + [VMEM] * 11,
        out_specs=[VMEM] * 5,
        scratch_shapes=[
            pltpu.VMEM((channels // LANES, (rows + 2 * H) * EXT, LANES), jnp.float32),
            pltpu.VMEM((rows * ROW, wide), jnp.bfloat16),
            pltpu.VMEM((rows * ROW, channels), jnp.bfloat16),
        ],
        compiler_params=pltpu.CompilerParams(vmem_limit_bytes=40 << 20),
        cost_estimate=pl.CostEstimate(flops=2_000_000_000, bytes_accessed=8_000_000, transcendentals=140_000),
    )(*lists, *around, upstream, weights)


def backward_kernel(b_pos, b_val, b_num, own, north, south, west, east, nw, ne, sw, se, upstream, weights,
                    state_grad, dext, dz):
    rows, width, channels = own.shape
    kcount = weights.shape[0] // channels
    room = b_pos.shape[0] // rows
    chunks = channels // LANES
    high = rows + 2 * H
    for q, w, mid, e, r in pieces(own, north, south, west, east, nw, ne, sw, se):
        base = q * EXT
        line = jnp.concatenate(
            [w[r], mid[r], e[r], jnp.zeros((EXT - 2 * LONREACH - width, channels), jnp.bfloat16)], axis=0
        )
        dext[base : base + EXT, :] = line
    for k in range(kcount):
        part = lax.dot_general(
            dext[...],
            weights[k * channels : (k + 1) * channels, :],
            (((1,), (1,)), ((), ())),
            preferred_element_type=jnp.float32,
        )
        part = part.astype(jnp.bfloat16).astype(jnp.float32)
        for c in range(chunks):
            dz[c, k * high * EXT : (k + 1) * high * EXT, :] = part[:, c * LANES : (c + 1) * LANES]
    for i in range(rows):
        for c in range(chunks):

            def add(n, acc):
                at = i * room + n
                return acc + b_val[at] * dz[c, pl.ds(b_pos[at], ROW), :]

            acc = lax.fori_loop(0, b_num[i], add, jnp.zeros((ROW, LANES), jnp.float32))
            lanes = slice(c * LANES, (c + 1) * LANES)
            adjoint = acc[:width].astype(jnp.bfloat16).astype(jnp.float32)
            state_grad[i, :, lanes] = (upstream[i, :, lanes].astype(jnp.float32) + adjoint).astype(jnp.bfloat16)


def backward(lists, around, upstream, weights):
    rows, width, channels = upstream.shape
    high = rows + 2 * H
    kcount = weights.shape[0] // channels
    return pl.pallas_call(
        backward_kernel,
        out_shape=jax.ShapeDtypeStruct((rows, width, channels), jnp.bfloat16),
        in_specs=[SMEM] * 3 + [VMEM] * 11,
        out_specs=VMEM,
        scratch_shapes=[
            pltpu.VMEM((high * EXT, channels), jnp.bfloat16),
            pltpu.VMEM((channels // LANES, kcount * high * EXT, LANES), jnp.float32),
        ],
        compiler_params=pltpu.CompilerParams(vmem_limit_bytes=40 << 20),
        cost_estimate=pl.CostEstimate(flops=2_500_000_000, bytes_accessed=5_000_000, transcendentals=0),
    )(*lists, *around, upstream, weights)


def around(block, west, east):
    lats, lons = lax.axis_size("lat"), lax.axis_size("lon")
    from_north = [(i, i + 1) for i in range(lats - 1)]
    from_south = [(i + 1, i) for i in range(lats - 1)]
    from_west = [(j, (j + 1) % lons) for j in range(lons)]
    from_east = [((j + 1) % lons, j) for j in range(lons)]

    def corner(lat_pairs, lon_pairs):
        return [(a * lons + c, b * lons + d) for a, b in lat_pairs for c, d in lon_pairs]

    north = lax.ppermute(block, "lat", from_north)
    south = lax.ppermute(block, "lat", from_south)
    w = lax.ppermute(east, "lon", from_west)
    e = lax.ppermute(west, "lon", from_east)
    both = ("lat", "lon")
    nw = lax.ppermute(east, both, corner(from_north, from_west))
    ne = lax.ppermute(west, both, corner(from_north, from_east))
    sw = lax.ppermute(east, both, corner(from_south, from_west))
    se = lax.ppermute(west, both, corner(from_south, from_east))
    return block, north, south, w, e, nw, ne, sw, se


def shards(state, cotangent, weights, lat_off, lon_off, basis, tap_val, tap_count):
    field, upstream = state[0], cotangent[0]
    rows, width, channels = field.shape
    wide = weights.reshape(-1, channels)
    lists = plan((lat_off, lon_off, basis, tap_val, tap_count), rows)
    near = around(field, field[:, :LONREACH], field[:, width - LONREACH :])
    new_field, dmixed, d_west, d_east, local_grad = forward(lists[:3], near, upstream, wide)
    summed = lax.psum(local_grad, ("dp", "lat", "lon"))
    cells = lax.axis_size("dp") * lax.axis_size("lat") * rows * lax.axis_size("lon") * width
    weight_grad = (summed / math.sqrt(cells)).astype(jnp.bfloat16).reshape(weights.shape)
    d_near = around(dmixed, d_west, d_east)
    field_grad = backward(lists[3:], d_near, upstream, wide)
    return new_field[None], field_grad[None], weight_grad


def solution(mesh):
    cells = P("dp", "lat", "lon", None)
    return jax.shard_map(
        shards,
        mesh=mesh,
        in_specs=(cells, cells, P(), P(), P(), P(), P(), P()),
        out_specs=(cells, cells, P()),
        check_vma=False,
    )
```

```python
import math

import jax
import jax.numpy as jnp
from jax import lax
from jax.experimental import pallas as pl
from jax.experimental.pallas import tpu as pltpu
from jax.sharding import PartitionSpec as P

H = 2
LONREACH = 24
RIM = 2 * LONREACH
LANES = 128
ROW = 192
EXT = ROW + RIM
SLOPE = math.sqrt(2.0 / math.pi)
CUBIC = 0.044715


SMEM = pl.BlockSpec(memory_space=pltpu.SMEM)
VMEM = pl.BlockSpec(memory_space=pltpu.VMEM)
HBM = pl.BlockSpec(memory_space=pltpu.HBM)
BF16, F32 = jnp.bfloat16, jnp.float32


def plan_kernel(lat_off, lon_off, basis, tap_val, tap_count, f_pos, f_val, b_pos, b_val, *, rows, kcount):
    taps, total = lat_off.shape
    high = rows + 2 * H
    first = lax.axis_index("lat") * rows
    for i in range(rows):
        row = first + i
        used = tap_count[row]
        slot = jnp.int32(0)
        for k in range(kcount):
            f_pos[rows * taps + i * 8 + k] = slot

            def add(t, slot):
                hit = basis[t, row] == k

                @pl.when(hit)
                def _():
                    f_pos[i * taps + slot] = (i + H + lat_off[t, row]) * EXT + LONREACH + lon_off[t, row]
                    f_val[i * taps + slot] = tap_val[t, row]

                return slot + hit.astype(jnp.int32)

            slot = lax.fori_loop(0, used, add, slot)
        f_pos[rows * taps + i * 8 + kcount] = slot
    room = high * taps
    counts = tuple(jnp.int32(0) for _ in range(rows))
    for e in range(high):
        row = first + (e - H)
        inside = (row >= 0) & (row < total)
        row = jnp.clip(row, 0, total - 1)
        used = jnp.where(inside, tap_count[row], 0)

        def give(t, counts):
            target = e - H + lat_off[t, row]
            new = []
            for i in range(rows):
                hit = target == i

                @pl.when(hit)
                def _():
                    at = i * room + counts[i]
                    b_pos[at] = (basis[t, row] * high + e) * EXT + LONREACH - lon_off[t, row]
                    b_val[at] = tap_val[t, row]

                new.append(counts[i] + hit.astype(jnp.int32))
            return tuple(new)

        counts = lax.fori_loop(0, used, give, counts)
    for i in range(rows):
        b_pos[rows * room + i] = counts[i]


def plan(tables, rows, kcount):
    taps = tables[0].shape[0]
    room = (rows + 2 * H) * taps

    def body(*refs):
        plan_kernel(*refs, rows=rows, kcount=kcount)

    return pl.pallas_call(
        body,
        out_shape=[
            jax.ShapeDtypeStruct((rows * taps + rows * 8,), jnp.int32),
            jax.ShapeDtypeStruct((rows * taps,), F32),
            jax.ShapeDtypeStruct((rows * room + 8,), jnp.int32),
            jax.ShapeDtypeStruct((rows * room,), F32),
        ],
        in_specs=[SMEM] * 5,
        out_specs=[SMEM] * 4,
    )(*tables)


def forward_kernel(pos_hbm, val_hbm, weights_hbm, own, north, south, east, ne, se, upstream,
                   new_state, dmixed, west_out, rim_out, grad, pos, val, weights, ext, up, z, dm, sems, *, scale):
    rows, width, channels = own.shape
    kcount = weights.shape[0] // channels
    taps = val.shape[0] // rows
    chunks = channels // LANES
    copies = [
        pltpu.make_async_copy(pos_hbm, pos, sems.at[0]),
        pltpu.make_async_copy(val_hbm, val, sems.at[1]),
        pltpu.make_async_copy(weights_hbm, weights, sems.at[2]),
    ]
    for copy in copies:
        copy.start()
    for side, (mid, rim) in enumerate(((north, ne), (own, east), (south, se))):
        for r in range(rows):
            base = (side * rows + r) * EXT
            for c in range(chunks):
                lanes = slice(c * LANES, (c + 1) * LANES)
                ext[c, base : base + width, :] = mid[r, :, lanes].astype(F32)
                ext[c, base + width : base + width + RIM, :] = rim[r, :RIM, lanes].astype(F32)
                ext[c, base + width + RIM : base + EXT, :] = jnp.zeros((EXT - RIM - width, LANES), F32)
    for i in range(rows):
        kept = width - LONREACH
        up[i, :kept] = upstream[i].astype(F32)[LONREACH:]
        up[i, kept:width] = east[i].astype(F32)[RIM:]
    copies[0].wait()
    copies[1].wait()
    for i in range(rows):
        for k in range(kcount):
            for c in range(chunks):

                def add(n, acc):
                    at = i * taps + n
                    return acc + val[at] * ext[c, pl.ds(pos[at], ROW), :]

                begin = pos[rows * taps + i * 8 + k]
                end = pos[rows * taps + i * 8 + k + 1]
                acc = lax.fori_loop(begin, end, add, jnp.zeros((ROW, LANES), F32))
                col = k * channels + c * LANES
                z[i * ROW : (i + 1) * ROW, col : col + LANES] = acc.astype(BF16)
    copies[2].wait()
    mixed = jnp.dot(z[...], weights[...], preferred_element_type=F32)
    for i in range(rows):
        x = mixed[i * ROW : i * ROW + width]
        square = x * x
        t = jnp.tanh(SLOPE * (x + CUBIC * (square * x)))
        cdf = 0.5 * (1.0 + t)
        base = (H + i) * EXT + LONREACH
        field = jnp.concatenate([ext[c, base : base + width, :] for c in range(chunks)], axis=1)
        made = (field + x * cdf).astype(BF16)
        slope = cdf + x * (0.5 * (1.0 - t * t)) * (SLOPE * (1.0 + (3.0 * CUBIC) * square))
        d = (up[i, :width] * slope).astype(BF16)
        new_state[i] = made
        dmixed[i] = d
        rim_out[i] = d[width - RIM :]
        west_out[i, :RIM] = d[width - RIM :]
        west_out[i, RIM:] = made[width - LONREACH :]
        dm[i * ROW : (i + 1) * ROW, :] = jnp.concatenate([d, jnp.zeros((ROW - width, channels), BF16)], axis=0)
    total = lax.dot_general(z[...], dm[...], (((0,), (0,)), ((), ())), preferred_element_type=F32)
    grad[...] = total * scale


def forward(lists, weights, fields, upstream, scale):
    rows, width, channels = upstream.shape
    wide = weights.shape[0]
    block = jax.ShapeDtypeStruct((rows, width, channels), BF16)

    def body(*refs):
        forward_kernel(*refs, scale=scale)

    return pl.pallas_call(
        body,
        out_shape=[
            block,
            block,
            jax.ShapeDtypeStruct((rows, RIM + LONREACH, channels), BF16),
            jax.ShapeDtypeStruct((rows, RIM, channels), BF16),
            jax.ShapeDtypeStruct((wide, channels), F32),
        ],
        in_specs=[HBM] * 3 + [VMEM] * 7,
        out_specs=[VMEM] * 5,
        scratch_shapes=[
            pltpu.SMEM(lists[0].shape, jnp.int32),
            pltpu.SMEM(lists[1].shape, F32),
            pltpu.VMEM(weights.shape, BF16),
            pltpu.VMEM((channels // LANES, (rows + 2 * H) * EXT, LANES), F32),
            pltpu.VMEM((rows, ROW, channels), F32),
            pltpu.VMEM((rows * ROW, wide), BF16),
            pltpu.VMEM((rows * ROW, channels), BF16),
            pltpu.SemaphoreType.DMA((3,)),
        ],
        compiler_params=pltpu.CompilerParams(vmem_limit_bytes=40 << 20),
        cost_estimate=pl.CostEstimate(flops=2_000_000_000, bytes_accessed=8_000_000, transcendentals=140_000),
    )(*lists, weights, *fields, upstream)


def backward_kernel(pos_hbm, val_hbm, weights_hbm, own, north, south, west, nw, sw, made, upstream,
                    new_state, state_grad, pos, val, weights, dext, dz, sems):
    rows, width, channels = own.shape
    kcount = weights.shape[0] // channels
    room = val.shape[0] // rows
    chunks = channels // LANES
    high = rows + 2 * H
    copies = [
        pltpu.make_async_copy(weights_hbm, weights, sems.at[2]),
        pltpu.make_async_copy(pos_hbm, pos, sems.at[0]),
        pltpu.make_async_copy(val_hbm, val, sems.at[1]),
    ]
    for copy in copies:
        copy.start()
    for side, (mid, rim) in enumerate(((north, nw), (own, west), (south, sw))):
        for r in range(rows):
            base = (side * rows + r) * EXT
            dext[base : base + RIM, :] = rim[r, :RIM]
            dext[base + RIM : base + EXT, :] = jnp.concatenate(
                [mid[r], jnp.zeros((EXT - RIM - width, channels), BF16)], axis=0
            )
    for i in range(rows):
        new_state[i] = jnp.concatenate([west[i, RIM:], made[i, : width - LONREACH]], axis=0)
    copies[0].wait()
    for k in range(kcount):
        part = lax.dot_general(
            dext[...],
            weights[k * channels : (k + 1) * channels, :],
            (((1,), (1,)), ((), ())),
            preferred_element_type=F32,
        )
        part = part.astype(BF16).astype(F32)
        for c in range(chunks):
            dz[c, k * high * EXT : (k + 1) * high * EXT, :] = part[:, c * LANES : (c + 1) * LANES]
    copies[1].wait()
    copies[2].wait()
    for i in range(rows):
        for c in range(chunks):

            def add(n, acc):
                at = i * room + n
                return acc + val[at] * dz[c, pl.ds(pos[at], ROW), :]

            acc = lax.fori_loop(0, pos[rows * room + i], add, jnp.zeros((ROW, LANES), F32))
            lanes = slice(c * LANES, (c + 1) * LANES)
            adjoint = acc[:width].astype(BF16).astype(F32)
            state_grad[i, :, lanes] = (upstream[i, :, lanes].astype(F32) + adjoint).astype(BF16)


def backward(lists, weights, fields, made, upstream):
    rows, width, channels = upstream.shape
    high = rows + 2 * H
    kcount = weights.shape[0] // channels
    block = jax.ShapeDtypeStruct((rows, width, channels), BF16)
    return pl.pallas_call(
        backward_kernel,
        out_shape=[block, block],
        in_specs=[HBM] * 3 + [VMEM] * 8,
        out_specs=[VMEM] * 2,
        scratch_shapes=[
            pltpu.SMEM(lists[0].shape, jnp.int32),
            pltpu.SMEM(lists[1].shape, F32),
            pltpu.VMEM(weights.shape, BF16),
            pltpu.VMEM((high * EXT, channels), BF16),
            pltpu.VMEM((channels // LANES, kcount * high * EXT, LANES), F32),
            pltpu.SemaphoreType.DMA((3,)),
        ],
        compiler_params=pltpu.CompilerParams(vmem_limit_bytes=40 << 20),
        cost_estimate=pl.CostEstimate(flops=2_500_000_000, bytes_accessed=5_000_000, transcendentals=0),
    )(*lists, weights, *fields, made, upstream)


def around(block, side, rim, step):
    lats, lons = lax.axis_size("lat"), lax.axis_size("lon")
    from_north = [(i, i + 1) for i in range(lats - 1)]
    from_south = [(i + 1, i) for i in range(lats - 1)]
    along = [(j, (j + step) % lons) for j in range(lons)]

    def corner(lat_pairs):
        return [(a * lons + c, b * lons + d) for a, b in lat_pairs for c, d in along]

    north = lax.ppermute(block, "lat", from_north)
    south = lax.ppermute(block, "lat", from_south)
    level = lax.ppermute(side, "lon", along)
    upper = lax.ppermute(rim, ("lat", "lon"), corner(from_north))
    lower = lax.ppermute(rim, ("lat", "lon"), corner(from_south))
    return block, north, south, level, upper, lower


def shards(state, cotangent, weights, lat_off, lon_off, basis, tap_val, tap_count):
    field, upstream = state[0], cotangent[0]
    rows, width, channels = field.shape
    kcount = weights.shape[0]
    wide = weights.reshape(-1, channels)
    side = jnp.concatenate([field[:, :RIM], upstream[:, :LONREACH]], axis=1)
    fields = around(field, side, field[:, :RIM], -1)
    lists = plan((lat_off.T, lon_off.T, basis.T, tap_val.T, tap_count), rows, kcount)
    cells = lax.axis_size("dp") * lax.axis_size("lat") * rows * lax.axis_size("lon") * width
    made, dmixed, side, rim, share = forward(lists[:2], wide, fields, upstream, 1.0 / math.sqrt(cells))
    fields = around(dmixed, side, rim, 1)
    weight_grad = lax.psum(share, ("dp", "lat", "lon")).astype(BF16).reshape(weights.shape)
    new_field, field_grad = backward(lists[2:], wide, fields, made, upstream)
    return new_field[None], field_grad[None], weight_grad


def solution(mesh):
    cells = P("dp", "lat", "lon", None)
    return jax.shard_map(
        shards,
        mesh=mesh,
        in_specs=(cells, cells, P(), P(), P(), P(), P(), P()),
        out_specs=(cells, cells, P()),
        check_vma=False,
    )
```

```python
import math

import jax
import jax.numpy as jnp
from jax import lax
from jax.experimental import pallas as pl
from jax.experimental.pallas import tpu as pltpu
from jax.sharding import PartitionSpec as P

H = 2
LONREACH = 24
RIM = 2 * LONREACH
LANES = 128
ROW = 192
EXT = ROW + RIM
SLOPE = math.sqrt(2.0 / math.pi)
CUBIC = 0.044715


SMEM = pl.BlockSpec(memory_space=pltpu.SMEM)
VMEM = pl.BlockSpec(memory_space=pltpu.VMEM)
BF16, F32 = jnp.bfloat16, jnp.float32
DP, LAT = ("x_hi", "core"), ("y", "x_lo")
ALONG_X = ("x_hi", "core", "x_lo")


def forward_taps(tables, first, rows, kcount, pos, val):
    lat_off, lon_off, basis, tap_val, tap_count = tables
    taps = lat_off.shape[0]
    room = taps + 1
    for i in range(rows):
        row = first + i
        used = tap_count[row]
        counts = [jnp.int32(0) for _ in range(kcount)]
        for t in range(taps):
            where = (i + H + lat_off[t, row]) * EXT + LONREACH + lon_off[t, row]
            value = tap_val[t, row]
            kind = jnp.where(t < used, basis[t, row], kcount)
            for k in range(kcount):
                at = (i * kcount + k) * room + counts[k]
                pos[at] = where
                val[at] = value
                counts[k] = counts[k] + (kind == k).astype(jnp.int32)
        for k in range(kcount):
            pos[rows * kcount * room + i * kcount + k] = counts[k]


def backward_taps(tables, first, rows, pos, val):
    lat_off, lon_off, basis, tap_val, tap_count = tables
    taps, total = lat_off.shape
    high = rows + 2 * H
    room = high * taps + 1
    counts = [jnp.int32(0) for _ in range(rows)]
    for e in range(high):
        row = first + (e - H)
        inside = (row >= 0) & (row < total)
        row = jnp.clip(row, 0, total - 1)
        used = jnp.where(inside, tap_count[row], 0)
        for t in range(taps):
            where = (basis[t, row] * high + e) * EXT + LONREACH - lon_off[t, row]
            value = tap_val[t, row]
            target = jnp.where(t < used, e - H + lat_off[t, row], -1)
            for i in range(rows):
                at = i * room + counts[i]
                pos[at] = where
                val[at] = value
                counts[i] = counts[i] + (target == i).astype(jnp.int32)
    for i in range(rows):
        pos[rows * room + i] = counts[i]


def forward_kernel(lat_off, lon_off, basis, tap_val, tap_count, weights, own, north, south, east, ne, se, upstream,
                   new_state, dmixed, west_out, rim_out, grad, pos, val, ext, up, z, dm, *, scale):
    rows, width, channels = own.shape
    kcount = weights.shape[0] // channels
    chunks = channels // LANES
    tables = (lat_off, lon_off, basis, tap_val, tap_count)
    room = lat_off.shape[0] + 1
    forward_taps(tables, lax.axis_index(LAT) * rows, rows, kcount, pos, val)
    for side, (mid, rim) in enumerate(((north, ne), (own, east), (south, se))):
        for r in range(rows):
            base = (side * rows + r) * EXT
            for c in range(chunks):
                lanes = slice(c * LANES, (c + 1) * LANES)
                ext[c, base : base + width, :] = mid[r, :, lanes].astype(F32)
                ext[c, base + width : base + width + RIM, :] = rim[r, :RIM, lanes].astype(F32)
                ext[c, base + width + RIM : base + EXT, :] = jnp.zeros((EXT - RIM - width, LANES), F32)
    for i in range(rows):
        kept = width - LONREACH
        up[i, :kept] = upstream[i].astype(F32)[LONREACH:]
        up[i, kept:width] = east[i].astype(F32)[RIM:]
    for i in range(rows):
        for k in range(kcount):
            for c in range(chunks):

                def add(n, acc):
                    at = (i * kcount + k) * room + n
                    return acc + val[at] * ext[c, pl.ds(pos[at], ROW), :]

                count = pos[rows * kcount * room + i * kcount + k]
                acc = lax.fori_loop(0, count, add, jnp.zeros((ROW, LANES), F32))
                col = k * channels + c * LANES
                z[i * ROW : (i + 1) * ROW, col : col + LANES] = acc.astype(BF16)
    mixed = jnp.dot(z[...], weights[...], preferred_element_type=F32)
    for i in range(rows):
        x = mixed[i * ROW : i * ROW + width]
        square = x * x
        t = jnp.tanh(SLOPE * (x + CUBIC * (square * x)))
        cdf = 0.5 * (1.0 + t)
        base = (H + i) * EXT + LONREACH
        field = jnp.concatenate([ext[c, base : base + width, :] for c in range(chunks)], axis=1)
        made = (field + x * cdf).astype(BF16)
        slope = cdf + x * (0.5 * (1.0 - t * t)) * (SLOPE * (1.0 + (3.0 * CUBIC) * square))
        d = (up[i, :width] * slope).astype(BF16)
        new_state[i] = made
        dmixed[i] = d
        rim_out[i] = d[width - RIM :]
        west_out[i, :RIM] = d[width - RIM :]
        west_out[i, RIM:] = made[width - LONREACH :]
        dm[i * ROW : (i + 1) * ROW, :] = jnp.concatenate([d, jnp.zeros((ROW - width, channels), BF16)], axis=0)
    total = lax.dot_general(z[...], dm[...], (((0,), (0,)), ((), ())), preferred_element_type=F32)
    grad[...] = (total * scale).astype(BF16)


def forward(tables, weights, fields, upstream, scale):
    rows, width, channels = upstream.shape
    wide = weights.shape[0]
    lists = rows * (wide // channels) * (tables[0].shape[0] + 1)
    block = jax.ShapeDtypeStruct((rows, width, channels), BF16)

    def body(*refs):
        forward_kernel(*refs, scale=scale)

    return pl.pallas_call(
        body,
        out_shape=[
            block,
            block,
            jax.ShapeDtypeStruct((rows, RIM + LONREACH, channels), BF16),
            jax.ShapeDtypeStruct((rows, RIM, channels), BF16),
            jax.ShapeDtypeStruct((wide, channels), BF16),
        ],
        in_specs=[SMEM] * 5 + [VMEM] * 8,
        out_specs=[VMEM] * 5,
        scratch_shapes=[
            pltpu.SMEM((lists + 64,), jnp.int32),
            pltpu.SMEM((lists,), F32),
            pltpu.VMEM((channels // LANES, (rows + 2 * H) * EXT, LANES), F32),
            pltpu.VMEM((rows, ROW, channels), F32),
            pltpu.VMEM((rows * ROW, wide), BF16),
            pltpu.VMEM((rows * ROW, channels), BF16),
        ],
        compiler_params=pltpu.CompilerParams(vmem_limit_bytes=24 << 20),
        cost_estimate=pl.CostEstimate(flops=2_000_000_000, bytes_accessed=8_000_000, transcendentals=140_000),
    )(*tables, weights, *fields, upstream)


def backward_kernel(lat_off, lon_off, basis, tap_val, tap_count, weights, own, north, south, west, nw, sw, made, upstream,
                    new_state, state_grad, pos, val, dext, dz):
    rows, width, channels = own.shape
    kcount = weights.shape[0] // channels
    chunks = channels // LANES
    high = rows + 2 * H
    tables = (lat_off, lon_off, basis, tap_val, tap_count)
    room = high * lat_off.shape[0] + 1
    backward_taps(tables, lax.axis_index(LAT) * rows, rows, pos, val)
    for side, (mid, rim) in enumerate(((north, nw), (own, west), (south, sw))):
        for r in range(rows):
            base = (side * rows + r) * EXT
            dext[base : base + RIM, :] = rim[r, :RIM]
            dext[base + RIM : base + EXT, :] = jnp.concatenate(
                [mid[r], jnp.zeros((EXT - RIM - width, channels), BF16)], axis=0
            )
    for i in range(rows):
        new_state[i] = jnp.concatenate([west[i, RIM:], made[i, : width - LONREACH]], axis=0)
    for k in range(kcount):
        part = lax.dot_general(
            dext[...],
            weights[k * channels : (k + 1) * channels, :],
            (((1,), (1,)), ((), ())),
            preferred_element_type=F32,
        )
        part = part.astype(BF16).astype(F32)
        for c in range(chunks):
            dz[c, k * high * EXT : (k + 1) * high * EXT, :] = part[:, c * LANES : (c + 1) * LANES]
    for i in range(rows):
        for c in range(chunks):

            def add(n, acc):
                at = i * room + n
                return acc + val[at] * dz[c, pl.ds(pos[at], ROW), :]

            acc = lax.fori_loop(0, pos[rows * room + i], add, jnp.zeros((ROW, LANES), F32))
            lanes = slice(c * LANES, (c + 1) * LANES)
            adjoint = acc[:width].astype(BF16).astype(F32)
            state_grad[i, :, lanes] = (upstream[i, :, lanes].astype(F32) + adjoint).astype(BF16)


def backward(tables, weights, fields, made, upstream):
    rows, width, channels = upstream.shape
    high = rows + 2 * H
    kcount = weights.shape[0] // channels
    lists = rows * (high * tables[0].shape[0] + 1)
    block = jax.ShapeDtypeStruct((rows, width, channels), BF16)
    return pl.pallas_call(
        backward_kernel,
        out_shape=[block, block],
        in_specs=[SMEM] * 5 + [VMEM] * 9,
        out_specs=[VMEM] * 2,
        scratch_shapes=[
            pltpu.SMEM((lists + 8,), jnp.int32),
            pltpu.SMEM((lists,), F32),
            pltpu.VMEM((high * EXT, channels), BF16),
            pltpu.VMEM((channels // LANES, kcount * high * EXT, LANES), F32),
        ],
        compiler_params=pltpu.CompilerParams(vmem_limit_bytes=24 << 20),
        cost_estimate=pl.CostEstimate(flops=2_500_000_000, bytes_accessed=5_000_000, transcendentals=0),
    )(*tables, weights, *fields, made, upstream)


def around(block, side, rim, step):
    lats, lons = lax.axis_size(LAT), lax.axis_size("lon")
    from_north = [(i, i + 1) for i in range(lats - 1)]
    from_south = [(i + 1, i) for i in range(lats - 1)]
    along = [(j, (j + step) % lons) for j in range(lons)]

    def corner(lat_pairs):
        return [(a * lons + c, b * lons + d) for a, b in lat_pairs for c, d in along]

    north = lax.ppermute(block, LAT, from_north)
    south = lax.ppermute(block, LAT, from_south)
    level = lax.ppermute(side, "lon", along)
    upper = lax.ppermute(rim, LAT + ("lon",), corner(from_north))
    lower = lax.ppermute(rim, LAT + ("lon",), corner(from_south))
    return block, north, south, level, upper, lower


def sum_pieces(pieces, out_shape, passed=()):
    def body(*refs):
        part, out = refs[0], refs[1 + len(passed)]
        total = part[0].astype(F32)
        for n in range(1, part.shape[0]):
            total = total + part[n].astype(F32)
        total = total.astype(out.dtype)
        if len(out.shape) == len(total.shape):
            out[...] = total
        else:
            for n in range(out.shape[0]):
                out[n] = total

    anywhere = pl.BlockSpec(memory_space=pl.ANY)
    return pl.pallas_call(
        body,
        out_shape=[out_shape] + [jax.ShapeDtypeStruct(x.shape, x.dtype) for x in passed],
        in_specs=[VMEM] + [anywhere] * len(passed),
        out_specs=[VMEM] + [anywhere] * len(passed),
        input_output_aliases={1 + n: 1 + n for n in range(len(passed))},
        compiler_params=pltpu.CompilerParams(vmem_limit_bytes=8 << 20),
    )(pieces, *passed)


def spread(block, copies, passed=()):
    def body(*refs):
        source, out = refs[0], refs[1 + len(passed)]
        for n in range(copies):
            out[n] = source[...]

    anywhere = pl.BlockSpec(memory_space=pl.ANY)
    return pl.pallas_call(
        body,
        out_shape=[jax.ShapeDtypeStruct((copies, *block.shape), block.dtype)]
        + [jax.ShapeDtypeStruct(x.shape, x.dtype) for x in passed],
        in_specs=[VMEM] + [anywhere] * len(passed),
        out_specs=[VMEM] + [anywhere] * len(passed),
        input_output_aliases={1 + n: 1 + n for n in range(len(passed))},
        compiler_params=pltpu.CompilerParams(vmem_limit_bytes=8 << 20),
    )(block, *passed)


def exchange(pieces, axes):
    return lax.all_to_all(pieces, axes, 0, 0, tiled=True)


def shards(state, cotangent, weights, lat_off, lon_off, basis, tap_val, tap_count):
    field, upstream = state[0], cotangent[0]
    rows, width, channels = field.shape
    kcount = weights.shape[0]
    wide = weights.reshape(-1, channels)
    tables = (lat_off.T, lon_off.T, basis.T, tap_val.T, tap_count)
    side = jnp.concatenate([field[:, :RIM], upstream[:, :LONREACH]], axis=1)
    fields = around(field, side, field[:, :RIM], -1)
    cells = lax.axis_size(DP) * lax.axis_size(LAT) * rows * lax.axis_size("lon") * width
    made, dmixed, side, rim, share = forward(tables, wide, fields, upstream, 1.0 / math.sqrt(cells))
    nx, ny, nz = lax.axis_size(ALONG_X), lax.axis_size("y"), lax.axis_size("lon")
    shape_x = (share.shape[0] // nx, channels)
    shape_y = (shape_x[0] // ny, channels)
    got = exchange(share.reshape(nx, *shape_x), ALONG_X)
    part, dmixed, side, rim = sum_pieces(got, jax.ShapeDtypeStruct(shape_x, F32), (dmixed, side, rim))
    got = exchange(part.reshape(ny, *shape_y), "y")
    fields = around(dmixed, side, rim, 1)
    (part,) = sum_pieces(got, jax.ShapeDtypeStruct((nz, *shape_y), F32))
    got = exchange(part, "lon")
    (part,) = sum_pieces(got, jax.ShapeDtypeStruct((ny, *shape_y), BF16))
    got = exchange(part, "y")
    new_field, field_grad = backward(tables, wide, fields, made, upstream)
    part, new_field, field_grad = spread(got.reshape(shape_x), nx, (new_field, field_grad))
    weight_grad = exchange(part, ALONG_X).reshape(weights.shape)
    return new_field[None], field_grad[None], weight_grad


def solution(mesh):
    dp, lat, lon = (mesh.shape[name] for name in ("dp", "lat", "lon"))
    finer = jax.sharding.Mesh(mesh.devices.reshape(dp // 2, 2, lat // 2, 2, lon), DP + ("y", "x_lo", "lon"))
    cells = P(DP, LAT, "lon", None)
    return jax.shard_map(
        shards,
        mesh=finer,
        in_specs=(cells, cells, P(), P(), P(), P(), P(), P()),
        out_specs=(cells, cells, P()),
        check_vma=False,
    )
```

```python
import math

import jax
import jax.numpy as jnp
from jax import lax
from jax.experimental import pallas as pl
from jax.experimental.pallas import tpu as pltpu
from jax.sharding import PartitionSpec as P

H = 2
LONREACH = 24
RIM = 2 * LONREACH
LANES = 128
ROW = 192
EXT = ROW + RIM
SLOPE = math.sqrt(2.0 / math.pi)
CUBIC = 0.044715


SMEM = pl.BlockSpec(memory_space=pltpu.SMEM)
VMEM = pl.BlockSpec(memory_space=pltpu.VMEM)
BF16, F32 = jnp.bfloat16, jnp.float32
DP, LAT = ("x_hi", "core"), ("y", "x_lo")
ALONG_X = ("x_hi", "core", "x_lo")


def forward_taps(tables, first, rows, kcount, pos, val):
    lat_off, lon_off, basis, tap_val, tap_count = tables
    taps = lat_off.shape[0]
    room = taps + 1
    for i in range(rows):
        row = first + i
        used = tap_count[row]
        counts = [jnp.int32(0) for _ in range(kcount)]
        for t in range(taps):
            where = (i + H + lat_off[t, row]) * EXT + LONREACH + lon_off[t, row]
            value = tap_val[t, row]
            kind = jnp.where(t < used, basis[t, row], kcount)
            for k in range(kcount):
                at = (i * kcount + k) * room + counts[k]
                pos[at] = where
                val[at] = value
                counts[k] = counts[k] + (kind == k).astype(jnp.int32)
        for k in range(kcount):
            pos[rows * kcount * room + i * kcount + k] = counts[k]


def backward_taps(tables, first, rows, pos, val):
    lat_off, lon_off, basis, tap_val, tap_count = tables
    taps, total = lat_off.shape
    high = rows + 2 * H
    room = high * taps + 1
    counts = [jnp.int32(0) for _ in range(rows)]
    for e in range(high):
        row = first + (e - H)
        inside = (row >= 0) & (row < total)
        row = jnp.clip(row, 0, total - 1)
        used = jnp.where(inside, tap_count[row], 0)
        for t in range(taps):
            where = (basis[t, row] * high + e) * EXT + LONREACH - lon_off[t, row]
            value = tap_val[t, row]
            target = jnp.where(t < used, e - H + lat_off[t, row], -1)
            for i in range(rows):
                at = i * room + counts[i]
                pos[at] = where
                val[at] = value
                counts[i] = counts[i] + (target == i).astype(jnp.int32)
    for i in range(rows):
        pos[rows * room + i] = counts[i]


def forward_kernel(lat_off, lon_off, basis, tap_val, tap_count, weights, own, north, south, east, ne, se, upstream,
                   new_state, dmixed, west_out, rim_out, grad, pos, val, ext, up, z, dm, *, scale):
    rows, width, channels = own.shape
    kcount = weights.shape[0] // channels
    chunks = channels // LANES
    tables = (lat_off, lon_off, basis, tap_val, tap_count)
    room = lat_off.shape[0] + 1
    forward_taps(tables, lax.axis_index(LAT) * rows, rows, kcount, pos, val)
    for side, (mid, rim) in enumerate(((north, ne), (own, east), (south, se))):
        for r in range(rows):
            base = (side * rows + r) * EXT
            for c in range(chunks):
                lanes = slice(c * LANES, (c + 1) * LANES)
                ext[c, base : base + width, :] = mid[r, :, lanes].astype(F32)
                ext[c, base + width : base + width + RIM, :] = rim[r, :RIM, lanes].astype(F32)
                ext[c, base + width + RIM : base + EXT, :] = jnp.zeros((EXT - RIM - width, LANES), F32)
    for i in range(rows):
        kept = width - LONREACH
        up[i, :kept] = upstream[i].astype(F32)[LONREACH:]
        up[i, kept:width] = east[i].astype(F32)[RIM:]
    for i in range(rows):
        for k in range(kcount):
            for c in range(chunks):

                def add(n, acc):
                    at = (i * kcount + k) * room + n
                    return acc + val[at] * ext[c, pl.ds(pos[at], ROW), :]

                count = pos[rows * kcount * room + i * kcount + k]
                acc = lax.fori_loop(0, count, add, jnp.zeros((ROW, LANES), F32))
                col = k * channels + c * LANES
                z[i * ROW : (i + 1) * ROW, col : col + LANES] = acc.astype(BF16)
    mixed = jnp.dot(z[...], weights[...], preferred_element_type=F32)
    for i in range(rows):
        x = mixed[i * ROW : i * ROW + width]
        square = x * x
        t = jnp.tanh(SLOPE * (x + CUBIC * (square * x)))
        cdf = 0.5 * (1.0 + t)
        base = (H + i) * EXT + LONREACH
        field = jnp.concatenate([ext[c, base : base + width, :] for c in range(chunks)], axis=1)
        made = (field + x * cdf).astype(BF16)
        slope = cdf + x * (0.5 * (1.0 - t * t)) * (SLOPE * (1.0 + (3.0 * CUBIC) * square))
        d = (up[i, :width] * slope).astype(BF16)
        new_state[i] = made
        dmixed[i] = d
        rim_out[i] = d[width - RIM :]
        west_out[i, :RIM] = d[width - RIM :]
        west_out[i, RIM:] = made[width - LONREACH :]
        dm[i * ROW : (i + 1) * ROW, :] = jnp.concatenate([d, jnp.zeros((ROW - width, channels), BF16)], axis=0)
    total = lax.dot_general(z[...], dm[...], (((0,), (0,)), ((), ())), preferred_element_type=F32)
    total = (total * scale).astype(BF16)
    for n in range(grad.shape[0]):
        grad[n] = total[n * grad.shape[1] : (n + 1) * grad.shape[1]]


def forward(tables, weights, fields, upstream, scale, shares):
    rows, width, channels = upstream.shape
    wide = weights.shape[0]
    lists = rows * (wide // channels) * (tables[0].shape[0] + 1)
    block = jax.ShapeDtypeStruct((rows, width, channels), BF16)

    def body(*refs):
        forward_kernel(*refs, scale=scale)

    return pl.pallas_call(
        body,
        out_shape=[
            block,
            block,
            jax.ShapeDtypeStruct((rows, RIM + LONREACH, channels), BF16),
            jax.ShapeDtypeStruct((rows, RIM, channels), BF16),
            jax.ShapeDtypeStruct((shares, wide // shares, channels), BF16),
        ],
        in_specs=[SMEM] * 5 + [VMEM] * 8,
        out_specs=[VMEM] * 5,
        scratch_shapes=[
            pltpu.SMEM((lists + 64,), jnp.int32),
            pltpu.SMEM((lists,), F32),
            pltpu.VMEM((channels // LANES, (rows + 2 * H) * EXT, LANES), F32),
            pltpu.VMEM((rows, ROW, channels), F32),
            pltpu.VMEM((rows * ROW, wide), BF16),
            pltpu.VMEM((rows * ROW, channels), BF16),
        ],
        compiler_params=pltpu.CompilerParams(vmem_limit_bytes=24 << 20),
        cost_estimate=pl.CostEstimate(flops=2_000_000_000, bytes_accessed=8_000_000, transcendentals=140_000),
    )(*tables, weights, *fields, upstream)


def backward_kernel(lat_off, lon_off, basis, tap_val, tap_count, weights, own, north, south, west, nw, sw, made, upstream,
                    new_state, state_grad, pos, val, dext, dz):
    rows, width, channels = own.shape
    kcount = weights.shape[0] // channels
    chunks = channels // LANES
    high = rows + 2 * H
    tables = (lat_off, lon_off, basis, tap_val, tap_count)
    room = high * lat_off.shape[0] + 1
    backward_taps(tables, lax.axis_index(LAT) * rows, rows, pos, val)
    for side, (mid, rim) in enumerate(((north, nw), (own, west), (south, sw))):
        for r in range(rows):
            base = (side * rows + r) * EXT
            dext[base : base + RIM, :] = rim[r, :RIM]
            dext[base + RIM : base + EXT, :] = jnp.concatenate(
                [mid[r], jnp.zeros((EXT - RIM - width, channels), BF16)], axis=0
            )
    for i in range(rows):
        new_state[i] = jnp.concatenate([west[i, RIM:], made[i, : width - LONREACH]], axis=0)
    for k in range(kcount):
        part = lax.dot_general(
            dext[...],
            weights[k * channels : (k + 1) * channels, :],
            (((1,), (1,)), ((), ())),
            preferred_element_type=F32,
        )
        part = part.astype(BF16).astype(F32)
        for c in range(chunks):
            dz[c, k * high * EXT : (k + 1) * high * EXT, :] = part[:, c * LANES : (c + 1) * LANES]
    for i in range(rows):
        for c in range(chunks):

            def add(n, acc):
                at = i * room + n
                return acc + val[at] * dz[c, pl.ds(pos[at], ROW), :]

            acc = lax.fori_loop(0, pos[rows * room + i], add, jnp.zeros((ROW, LANES), F32))
            lanes = slice(c * LANES, (c + 1) * LANES)
            adjoint = acc[:width].astype(BF16).astype(F32)
            state_grad[i, :, lanes] = (upstream[i, :, lanes].astype(F32) + adjoint).astype(BF16)


def backward(tables, weights, fields, made, upstream):
    rows, width, channels = upstream.shape
    high = rows + 2 * H
    kcount = weights.shape[0] // channels
    lists = rows * (high * tables[0].shape[0] + 1)
    block = jax.ShapeDtypeStruct((rows, width, channels), BF16)
    return pl.pallas_call(
        backward_kernel,
        out_shape=[block, block],
        in_specs=[SMEM] * 5 + [VMEM] * 9,
        out_specs=[VMEM] * 2,
        scratch_shapes=[
            pltpu.SMEM((lists + 8,), jnp.int32),
            pltpu.SMEM((lists,), F32),
            pltpu.VMEM((high * EXT, channels), BF16),
            pltpu.VMEM((channels // LANES, kcount * high * EXT, LANES), F32),
        ],
        compiler_params=pltpu.CompilerParams(vmem_limit_bytes=24 << 20),
        cost_estimate=pl.CostEstimate(flops=2_500_000_000, bytes_accessed=5_000_000, transcendentals=0),
    )(*tables, weights, *fields, made, upstream)


def around(block, side, rim, step):
    lats, lons = lax.axis_size(LAT), lax.axis_size("lon")
    from_north = [(i, i + 1) for i in range(lats - 1)]
    from_south = [(i + 1, i) for i in range(lats - 1)]
    along = [(j, (j + step) % lons) for j in range(lons)]

    def corner(lat_pairs):
        return [(a * lons + c, b * lons + d) for a, b in lat_pairs for c, d in along]

    north = lax.ppermute(block, LAT, from_north)
    south = lax.ppermute(block, LAT, from_south)
    level = lax.ppermute(side, "lon", along)
    upper = lax.ppermute(rim, LAT + ("lon",), corner(from_north))
    lower = lax.ppermute(rim, LAT + ("lon",), corner(from_south))
    return block, north, south, level, upper, lower


def sum_pieces(pieces, out_shape, passed=()):
    def body(*refs):
        part, out = refs[0], refs[1 + len(passed)]
        total = part[0].astype(F32)
        for n in range(1, part.shape[0]):
            total = total + part[n].astype(F32)
        total = total.astype(out.dtype)
        rows = out.shape[1]
        for n in range(out.shape[0]):
            out[n] = total if rows == total.shape[0] else total[n * rows : (n + 1) * rows]

    anywhere = pl.BlockSpec(memory_space=pl.ANY)
    return pl.pallas_call(
        body,
        out_shape=[out_shape] + [jax.ShapeDtypeStruct(x.shape, x.dtype) for x in passed],
        in_specs=[VMEM] + [anywhere] * len(passed),
        out_specs=[VMEM] + [anywhere] * len(passed),
        input_output_aliases={1 + n: 1 + n for n in range(len(passed))},
        compiler_params=pltpu.CompilerParams(vmem_limit_bytes=8 << 20),
    )(pieces, *passed)


def spread(block, copies, passed=()):
    def body(*refs):
        source, out = refs[0], refs[1 + len(passed)]
        for n in range(copies):
            out[n] = source[...]

    anywhere = pl.BlockSpec(memory_space=pl.ANY)
    return pl.pallas_call(
        body,
        out_shape=[jax.ShapeDtypeStruct((copies, *block.shape), block.dtype)]
        + [jax.ShapeDtypeStruct(x.shape, x.dtype) for x in passed],
        in_specs=[VMEM] + [anywhere] * len(passed),
        out_specs=[VMEM] + [anywhere] * len(passed),
        input_output_aliases={1 + n: 1 + n for n in range(len(passed))},
        compiler_params=pltpu.CompilerParams(vmem_limit_bytes=8 << 20),
    )(block, *passed)


def exchange(pieces, axes):
    return lax.all_to_all(pieces, axes, 0, 0, tiled=True)


def shards(state, cotangent, weights, lat_off, lon_off, basis, tap_val, tap_count):
    field, upstream = state[0], cotangent[0]
    rows, width, channels = field.shape
    kcount = weights.shape[0]
    wide = weights.reshape(-1, channels)
    tables = (lat_off.T, lon_off.T, basis.T, tap_val.T, tap_count)
    side = jnp.concatenate([field[:, :RIM], upstream[:, :LONREACH]], axis=1)
    fields = around(field, side, field[:, :RIM], -1)
    cells = lax.axis_size(DP) * lax.axis_size(LAT) * rows * lax.axis_size("lon") * width
    nx, ny, nz = lax.axis_size(ALONG_X), lax.axis_size("y"), lax.axis_size("lon")
    made, dmixed, side, rim, share = forward(tables, wide, fields, upstream, 1.0 / math.sqrt(cells), nx)
    piece = (wide.shape[0] // (nx * ny), channels)
    got = exchange(share, ALONG_X)
    fields = around(dmixed, side, rim, 1)
    part, *near = sum_pieces(got, jax.ShapeDtypeStruct((ny, *piece), F32), fields[1:])
    fields = (dmixed, *near)
    got = exchange(part, "y")
    (part,) = sum_pieces(got, jax.ShapeDtypeStruct((nz, *piece), F32))
    got = exchange(part, "lon")
    (part,) = sum_pieces(got, jax.ShapeDtypeStruct((ny, *piece), BF16))
    got = exchange(part, "y")
    new_field, field_grad = backward(tables, wide, fields, made, upstream)
    part, new_field, field_grad = spread(got.reshape(-1, channels), nx, (new_field, field_grad))
    weight_grad = exchange(part, ALONG_X).reshape(weights.shape)
    return new_field[None], field_grad[None], weight_grad


def solution(mesh):
    dp, lat, lon = (mesh.shape[name] for name in ("dp", "lat", "lon"))
    finer = jax.sharding.Mesh(mesh.devices.reshape(dp // 2, 2, lat // 2, 2, lon), DP + ("y", "x_lo", "lon"))
    cells = P(DP, LAT, "lon", None)
    return jax.shard_map(
        shards,
        mesh=finer,
        in_specs=(cells, cells, P(), P(), P(), P(), P(), P()),
        out_specs=(cells, cells, P()),
        check_vma=False,
    )
```

```python
import math

import jax
import jax.numpy as jnp
from jax import lax
from jax.experimental import pallas as pl
from jax.experimental.pallas import tpu as pltpu
from jax.sharding import PartitionSpec as P

H = 2
LONREACH = 24
RIM = 2 * LONREACH
LANES = 128
ROW = 192
EXT = ROW + RIM
SLOPE = math.sqrt(2.0 / math.pi)
CUBIC = 0.044715


SMEM = pl.BlockSpec(memory_space=pltpu.SMEM)
VMEM = pl.BlockSpec(memory_space=pltpu.VMEM)
BF16, F32 = jnp.bfloat16, jnp.float32
DP, LAT = ("x_hi", "core"), ("y", "x_lo")
ALONG_X = ("x_hi", "core", "x_lo")


def forward_taps(tables, first, rows, kcount, pos, val):
    lat_off, lon_off, basis, tap_val, tap_count = tables
    taps = lat_off.shape[0]
    room = taps + 1
    for i in range(rows):
        row = first + i
        used = tap_count[row]
        counts = [jnp.int32(0) for _ in range(kcount)]
        for t in range(taps):
            where = (i + H + lat_off[t, row]) * EXT + LONREACH + lon_off[t, row]
            value = tap_val[t, row]
            kind = jnp.where(t < used, basis[t, row], kcount)
            for k in range(kcount):
                at = (i * kcount + k) * room + counts[k]
                pos[at] = where
                val[at] = value
                counts[k] = counts[k] + (kind == k).astype(jnp.int32)
        for k in range(kcount):
            pos[rows * kcount * room + i * kcount + k] = counts[k]


def backward_taps(tables, first, rows, pos, val):
    lat_off, lon_off, basis, tap_val, tap_count = tables
    taps, total = lat_off.shape
    high = rows + 2 * H
    room = high * taps + 1
    counts = [jnp.int32(0) for _ in range(rows)]
    for e in range(high):
        row = first + (e - H)
        inside = (row >= 0) & (row < total)
        row = jnp.clip(row, 0, total - 1)
        used = jnp.where(inside, tap_count[row], 0)
        for t in range(taps):
            where = (basis[t, row] * high + e) * EXT + LONREACH - lon_off[t, row]
            value = tap_val[t, row]
            target = jnp.where(t < used, e - H + lat_off[t, row], -1)
            for i in range(rows):
                at = i * room + counts[i]
                pos[at] = where
                val[at] = value
                counts[i] = counts[i] + (target == i).astype(jnp.int32)
    for i in range(rows):
        pos[rows * room + i] = counts[i]


def forward_kernel(lat_off, lon_off, basis, tap_val, tap_count, weights, own, north, south, east, ne, se, upstream,
                   new_state, dmixed, west_out, rim_out, grad, pos, val, ext, up, z, dm, *, scale):
    rows, width, channels = own.shape
    kcount = weights.shape[0] // channels
    chunks = channels // LANES
    tables = (lat_off, lon_off, basis, tap_val, tap_count)
    room = lat_off.shape[0] + 1
    forward_taps(tables, lax.axis_index(LAT) * rows, rows, kcount, pos, val)
    for side, (mid, rim) in enumerate(((north, ne), (own, east), (south, se))):
        for r in range(rows):
            base = (side * rows + r) * EXT
            for c in range(chunks):
                lanes = slice(c * LANES, (c + 1) * LANES)
                ext[c, base : base + width, :] = mid[r, :, lanes].astype(F32)
                ext[c, base + width : base + width + RIM, :] = rim[r, :RIM, lanes].astype(F32)
                ext[c, base + width + RIM : base + EXT, :] = jnp.zeros((EXT - RIM - width, LANES), F32)
    for i in range(rows):
        kept = width - LONREACH
        up[i, :kept] = upstream[i].astype(F32)[LONREACH:]
        up[i, kept:width] = east[i].astype(F32)[RIM:]
    for i in range(rows):
        for k in range(kcount):
            for c in range(chunks):

                def add(n, acc):
                    at = (i * kcount + k) * room + n
                    return acc + val[at] * ext[c, pl.ds(pos[at], ROW), :]

                count = pos[rows * kcount * room + i * kcount + k]
                acc = lax.fori_loop(0, count, add, jnp.zeros((ROW, LANES), F32))
                col = k * channels + c * LANES
                z[i * ROW : (i + 1) * ROW, col : col + LANES] = acc.astype(BF16)
    mixed = jnp.dot(z[...], weights[...], preferred_element_type=F32)
    for i in range(rows):
        x = mixed[i * ROW : i * ROW + width]
        square = x * x
        t = jnp.tanh(SLOPE * (x + CUBIC * (square * x)))
        cdf = 0.5 * (1.0 + t)
        base = (H + i) * EXT + LONREACH
        field = jnp.concatenate([ext[c, base : base + width, :] for c in range(chunks)], axis=1)
        made = (field + x * cdf).astype(BF16)
        slope = cdf + x * (0.5 * (1.0 - t * t)) * (SLOPE * (1.0 + (3.0 * CUBIC) * square))
        d = (up[i, :width] * slope).astype(BF16)
        new_state[i] = made
        dmixed[i] = d
        rim_out[i] = d[width - RIM :]
        west_out[i, :RIM] = d[width - RIM :]
        west_out[i, RIM:] = made[width - LONREACH :]
        dm[i * ROW : (i + 1) * ROW, :] = jnp.concatenate([d, jnp.zeros((ROW - width, channels), BF16)], axis=0)
    total = lax.dot_general(z[...], dm[...], (((0,), (0,)), ((), ())), preferred_element_type=F32)
    total = (total * scale).astype(BF16)
    for n in range(grad.shape[0]):
        grad[n] = total[n * grad.shape[1] : (n + 1) * grad.shape[1]]


def forward(tables, weights, fields, upstream, scale, shares):
    rows, width, channels = upstream.shape
    wide = weights.shape[0]
    lists = rows * (wide // channels) * (tables[0].shape[0] + 1)
    block = jax.ShapeDtypeStruct((rows, width, channels), BF16)

    def body(*refs):
        forward_kernel(*refs, scale=scale)

    return pl.pallas_call(
        body,
        out_shape=[
            block,
            block,
            jax.ShapeDtypeStruct((rows, RIM + LONREACH, channels), BF16),
            jax.ShapeDtypeStruct((rows, RIM, channels), BF16),
            jax.ShapeDtypeStruct((shares, wide // shares, channels), BF16),
        ],
        in_specs=[SMEM] * 5 + [VMEM] * 8,
        out_specs=[VMEM] * 5,
        scratch_shapes=[
            pltpu.SMEM((lists + 64,), jnp.int32),
            pltpu.SMEM((lists,), F32),
            pltpu.VMEM((channels // LANES, (rows + 2 * H) * EXT, LANES), F32),
            pltpu.VMEM((rows, ROW, channels), F32),
            pltpu.VMEM((rows * ROW, wide), BF16),
            pltpu.VMEM((rows * ROW, channels), BF16),
        ],
        compiler_params=pltpu.CompilerParams(vmem_limit_bytes=24 << 20),
        cost_estimate=pl.CostEstimate(flops=2_000_000_000, bytes_accessed=8_000_000, transcendentals=140_000),
    )(*tables, weights, *fields, upstream)


def backward_kernel(lat_off, lon_off, basis, tap_val, tap_count, weights, own, north, south, west, nw, sw, made, upstream,
                    new_state, state_grad, pos, val, dext, dz):
    rows, width, channels = own.shape
    kcount = weights.shape[0] // channels
    chunks = channels // LANES
    high = rows + 2 * H
    tables = (lat_off, lon_off, basis, tap_val, tap_count)
    room = high * lat_off.shape[0] + 1
    backward_taps(tables, lax.axis_index(LAT) * rows, rows, pos, val)
    for side, (mid, rim) in enumerate(((north, nw), (own, west), (south, sw))):
        for r in range(rows):
            base = (side * rows + r) * EXT
            dext[base : base + RIM, :] = rim[r, :RIM]
            dext[base + RIM : base + EXT, :] = jnp.concatenate(
                [mid[r], jnp.zeros((EXT - RIM - width, channels), BF16)], axis=0
            )
    for i in range(rows):
        new_state[i] = jnp.concatenate([west[i, RIM:], made[i, : width - LONREACH]], axis=0)
    for k in range(kcount):
        part = lax.dot_general(
            dext[...],
            weights[k * channels : (k + 1) * channels, :],
            (((1,), (1,)), ((), ())),
            preferred_element_type=F32,
        )
        part = part.astype(BF16).astype(F32)
        for c in range(chunks):
            dz[c, k * high * EXT : (k + 1) * high * EXT, :] = part[:, c * LANES : (c + 1) * LANES]
    for i in range(rows):
        for c in range(chunks):

            def add(n, acc):
                at = i * room + n
                return acc + val[at] * dz[c, pl.ds(pos[at], ROW), :]

            acc = lax.fori_loop(0, pos[rows * room + i], add, jnp.zeros((ROW, LANES), F32))
            lanes = slice(c * LANES, (c + 1) * LANES)
            adjoint = acc[:width].astype(BF16).astype(F32)
            state_grad[i, :, lanes] = (upstream[i, :, lanes].astype(F32) + adjoint).astype(BF16)


def backward(tables, weights, fields, made, upstream):
    rows, width, channels = upstream.shape
    high = rows + 2 * H
    kcount = weights.shape[0] // channels
    lists = rows * (high * tables[0].shape[0] + 1)
    block = jax.ShapeDtypeStruct((rows, width, channels), BF16)
    return pl.pallas_call(
        backward_kernel,
        out_shape=[block, block],
        in_specs=[SMEM] * 5 + [VMEM] * 9,
        out_specs=[VMEM] * 2,
        scratch_shapes=[
            pltpu.SMEM((lists + 8,), jnp.int32),
            pltpu.SMEM((lists,), F32),
            pltpu.VMEM((high * EXT, channels), BF16),
            pltpu.VMEM((channels // LANES, kcount * high * EXT, LANES), F32),
        ],
        compiler_params=pltpu.CompilerParams(vmem_limit_bytes=24 << 20),
        cost_estimate=pl.CostEstimate(flops=2_500_000_000, bytes_accessed=5_000_000, transcendentals=0),
    )(*tables, weights, *fields, made, upstream)


def lat_blocks(block):
    ends = lax.axis_size(LAT) - 1
    north = lax.ppermute(block, LAT, [(i, i + 1) for i in range(ends)])
    south = lax.ppermute(block, LAT, [(i + 1, i) for i in range(ends)])
    return north, south


def lon_strips(side, rim, step):
    ends, lons = lax.axis_size(LAT) - 1, lax.axis_size("lon")
    along = [(j, (j + step) % lons) for j in range(lons)]
    level = lax.ppermute(side, "lon", along)
    upper = lax.ppermute(rim, LAT + ("lon",), [(i * lons + c, (i + 1) * lons + d) for i in range(ends) for c, d in along])
    lower = lax.ppermute(rim, LAT + ("lon",), [((i + 1) * lons + c, i * lons + d) for i in range(ends) for c, d in along])
    return level, upper, lower


def sum_pieces(pieces, out_shape, passed=()):
    def body(*refs):
        part, out = refs[0], refs[1 + len(passed)]
        total = part[0].astype(F32)
        for n in range(1, part.shape[0]):
            total = total + part[n].astype(F32)
        total = total.astype(out.dtype)
        rows = out.shape[1]
        for n in range(out.shape[0]):
            out[n] = total if rows == total.shape[0] else total[n * rows : (n + 1) * rows]

    anywhere = pl.BlockSpec(memory_space=pl.ANY)
    return pl.pallas_call(
        body,
        out_shape=[out_shape] + [jax.ShapeDtypeStruct(x.shape, x.dtype) for x in passed],
        in_specs=[VMEM] + [anywhere] * len(passed),
        out_specs=[VMEM] + [anywhere] * len(passed),
        input_output_aliases={1 + n: 1 + n for n in range(len(passed))},
        compiler_params=pltpu.CompilerParams(vmem_limit_bytes=8 << 20),
    )(pieces, *passed)


def spread(block, copies, passed=()):
    def body(*refs):
        source, out = refs[0], refs[1 + len(passed)]
        for n in range(copies):
            out[n] = source[...]

    anywhere = pl.BlockSpec(memory_space=pl.ANY)
    return pl.pallas_call(
        body,
        out_shape=[jax.ShapeDtypeStruct((copies, *block.shape), block.dtype)]
        + [jax.ShapeDtypeStruct(x.shape, x.dtype) for x in passed],
        in_specs=[VMEM] + [anywhere] * len(passed),
        out_specs=[VMEM] + [anywhere] * len(passed),
        input_output_aliases={1 + n: 1 + n for n in range(len(passed))},
        compiler_params=pltpu.CompilerParams(vmem_limit_bytes=8 << 20),
    )(block, *passed)


def exchange(pieces, axes):
    return lax.all_to_all(pieces, axes, 0, 0, tiled=True)


def shards(state, cotangent, weights, lat_off, lon_off, basis, tap_val, tap_count):
    field, upstream = state[0], cotangent[0]
    rows, width, channels = field.shape
    kcount = weights.shape[0]
    wide = weights.reshape(-1, channels)
    tables = (lat_off.T, lon_off.T, basis.T, tap_val.T, tap_count)
    side = jnp.concatenate([field[:, :RIM], upstream[:, :LONREACH]], axis=1)
    fields = (field, *lat_blocks(field), *lon_strips(side, field[:, :RIM], -1))
    cells = lax.axis_size(DP) * lax.axis_size(LAT) * rows * lax.axis_size("lon") * width
    nx, ny, nz = lax.axis_size(ALONG_X), lax.axis_size("y"), lax.axis_size("lon")
    made, dmixed, side, rim, share = forward(tables, wide, fields, upstream, 1.0 / math.sqrt(cells), nx)
    piece = (wide.shape[0] // (nx * ny), channels)
    got = exchange(share, ALONG_X)
    (part,) = sum_pieces(got, jax.ShapeDtypeStruct((ny, *piece), BF16))
    got = exchange(part, "y")
    part, dmixed = sum_pieces(got, jax.ShapeDtypeStruct((nz, *piece), F32), (dmixed,))
    blocks = lat_blocks(dmixed)
    got = exchange(part, "lon")
    part, side, rim = sum_pieces(got, jax.ShapeDtypeStruct((ny, *piece), BF16), (side, rim))
    strips = lon_strips(side, rim, 1)
    got = exchange(part, "y")
    part, *near = spread(got.reshape(-1, channels), nx, (*blocks, *strips))
    weight_grad = exchange(part, ALONG_X).reshape(weights.shape)
    new_field, field_grad = backward(tables, wide, (dmixed, *near), made, upstream)
    return new_field[None], field_grad[None], weight_grad


def solution(mesh):
    dp, lat, lon = (mesh.shape[name] for name in ("dp", "lat", "lon"))
    finer = jax.sharding.Mesh(mesh.devices.reshape(dp // 2, 2, lat // 2, 2, lon), DP + ("y", "x_lo", "lon"))
    cells = P(DP, LAT, "lon", None)
    return jax.shard_map(
        shards,
        mesh=finer,
        in_specs=(cells, cells, P(), P(), P(), P(), P(), P()),
        out_specs=(cells, cells, P()),
        check_vma=False,
    )
```

```python
import math

import jax
import jax.numpy as jnp
from jax import lax
from jax.experimental import pallas as pl
from jax.experimental.pallas import tpu as pltpu
from jax.sharding import PartitionSpec as P

H = 2
LONREACH = 24
RIM = 2 * LONREACH
LANES = 128
ROW = 192
EXT = ROW + RIM
SLOPE = math.sqrt(2.0 / math.pi)
CUBIC = 0.044715


SMEM = pl.BlockSpec(memory_space=pltpu.SMEM)
VMEM = pl.BlockSpec(memory_space=pltpu.VMEM)
BF16, F32 = jnp.bfloat16, jnp.float32
DP, LAT = ("x_hi", "core"), ("y", "x_lo")
ALONG_X = ("x_hi", "x_lo")


def forward_taps(tables, first, rows, kcount, pos, val):
    lat_off, lon_off, basis, tap_val, tap_count = tables
    taps = lat_off.shape[0]
    room = taps + 1
    for i in range(rows):
        row = first + i
        used = tap_count[row]
        counts = [jnp.int32(0) for _ in range(kcount)]
        for t in range(taps):
            where = (i + H + lat_off[t, row]) * EXT + LONREACH + lon_off[t, row]
            value = tap_val[t, row]
            kind = jnp.where(t < used, basis[t, row], kcount)
            for k in range(kcount):
                at = (i * kcount + k) * room + counts[k]
                pos[at] = where
                val[at] = value
                counts[k] = counts[k] + (kind == k).astype(jnp.int32)
        for k in range(kcount):
            pos[rows * kcount * room + i * kcount + k] = counts[k]


def backward_taps(tables, first, rows, pos, val):
    lat_off, lon_off, basis, tap_val, tap_count = tables
    taps, total = lat_off.shape
    high = rows + 2 * H
    room = high * taps + 1
    counts = [jnp.int32(0) for _ in range(rows)]
    for e in range(high):
        row = first + (e - H)
        inside = (row >= 0) & (row < total)
        row = jnp.clip(row, 0, total - 1)
        used = jnp.where(inside, tap_count[row], 0)
        for t in range(taps):
            where = (basis[t, row] * high + e) * EXT + LONREACH - lon_off[t, row]
            value = tap_val[t, row]
            target = jnp.where(t < used, e - H + lat_off[t, row], -1)
            for i in range(rows):
                at = i * room + counts[i]
                pos[at] = where
                val[at] = value
                counts[i] = counts[i] + (target == i).astype(jnp.int32)
    for i in range(rows):
        pos[rows * room + i] = counts[i]


def forward_kernel(lat_off, lon_off, basis, tap_val, tap_count, weights, own, north, south, east, ne, se, upstream,
                   new_state, dmixed, keep, send, pos, val, ext, up, z, dm, *, scale):
    rows, width, channels = own.shape
    kcount = weights.shape[0] // channels
    chunks = channels // LANES
    tables = (lat_off, lon_off, basis, tap_val, tap_count)
    room = lat_off.shape[0] + 1
    forward_taps(tables, lax.axis_index(LAT) * rows, rows, kcount, pos, val)
    for side, (mid, rim) in enumerate(((north, ne), (own, east), (south, se))):
        for r in range(rows):
            base = (side * rows + r) * EXT
            for c in range(chunks):
                lanes = slice(c * LANES, (c + 1) * LANES)
                ext[c, base : base + width, :] = mid[r, :, lanes].astype(F32)
                ext[c, base + width : base + width + RIM, :] = rim[r, :RIM, lanes].astype(F32)
                ext[c, base + width + RIM : base + EXT, :] = jnp.zeros((EXT - RIM - width, LANES), F32)
    for i in range(rows):
        kept = width - LONREACH
        up[i, :kept] = upstream[i].astype(F32)[LONREACH:]
        up[i, kept:width] = east[i].astype(F32)[RIM:]
    for i in range(rows):
        for k in range(kcount):
            for c in range(chunks):

                def add(n, acc):
                    at = (i * kcount + k) * room + n
                    return acc + val[at] * ext[c, pl.ds(pos[at], ROW), :]

                count = pos[rows * kcount * room + i * kcount + k]
                acc = lax.fori_loop(0, count, add, jnp.zeros((ROW, LANES), F32))
                col = k * channels + c * LANES
                z[i * ROW : (i + 1) * ROW, col : col + LANES] = acc.astype(BF16)
    mixed = jnp.dot(z[...], weights[...], preferred_element_type=F32)
    for i in range(rows):
        x = mixed[i * ROW : i * ROW + width]
        square = x * x
        t = jnp.tanh(SLOPE * (x + CUBIC * (square * x)))
        cdf = 0.5 * (1.0 + t)
        base = (H + i) * EXT + LONREACH
        field = jnp.concatenate([ext[c, base : base + width, :] for c in range(chunks)], axis=1)
        made = (field + x * cdf).astype(BF16)
        slope = cdf + x * (0.5 * (1.0 - t * t)) * (SLOPE * (1.0 + (3.0 * CUBIC) * square))
        d = (up[i, :width] * slope).astype(BF16)
        new_state[i] = made
        dmixed[i] = d
        dm[i * ROW : (i + 1) * ROW, :] = jnp.concatenate([d, jnp.zeros((ROW - width, channels), BF16)], axis=0)
    total = lax.dot_general(z[...], dm[...], (((0,), (0,)), ((), ())), preferred_element_type=F32)
    total = total * scale
    half = keep.shape[0]
    first = lax.axis_index("core") == 0
    keep[...] = jnp.where(first, total[:half], total[half:])
    send[...] = jnp.where(first, total[half:], total[:half]).astype(BF16)


def forward(tables, weights, fields, upstream, scale):
    rows, width, channels = upstream.shape
    wide = weights.shape[0]
    lists = rows * (wide // channels) * (tables[0].shape[0] + 1)
    block = jax.ShapeDtypeStruct((rows, width, channels), BF16)

    def body(*refs):
        forward_kernel(*refs, scale=scale)

    return pl.pallas_call(
        body,
        out_shape=[
            block,
            block,
            jax.ShapeDtypeStruct((wide // 2, channels), F32),
            jax.ShapeDtypeStruct((wide // 2, channels), BF16),
        ],
        in_specs=[SMEM] * 5 + [VMEM] * 8,
        out_specs=[VMEM] * 4,
        scratch_shapes=[
            pltpu.SMEM((lists + 64,), jnp.int32),
            pltpu.SMEM((lists,), F32),
            pltpu.VMEM((channels // LANES, (rows + 2 * H) * EXT, LANES), F32),
            pltpu.VMEM((rows, ROW, channels), F32),
            pltpu.VMEM((rows * ROW, wide), BF16),
            pltpu.VMEM((rows * ROW, channels), BF16),
        ],
        compiler_params=pltpu.CompilerParams(vmem_limit_bytes=24 << 20),
        cost_estimate=pl.CostEstimate(flops=2_000_000_000, bytes_accessed=8_000_000, transcendentals=140_000),
    )(*tables, weights, *fields, upstream)


def backward_kernel(lat_off, lon_off, basis, tap_val, tap_count, weights, own, north, south, strip, made, upstream,
                    new_state, state_grad, pos, val, dext, dz):
    rows, width, channels = own.shape
    kcount = weights.shape[0] // channels
    chunks = channels // LANES
    high = rows + 2 * H
    tables = (lat_off, lon_off, basis, tap_val, tap_count)
    room = high * lat_off.shape[0] + 1
    backward_taps(tables, lax.axis_index(LAT) * rows, rows, pos, val)
    for side, (mid, at) in enumerate(((north, 0), (own, 2 * RIM), (south, RIM))):
        for r in range(rows):
            base = (side * rows + r) * EXT
            dext[base : base + RIM, :] = strip[r, at : at + RIM]
            dext[base + RIM : base + EXT, :] = jnp.concatenate(
                [mid[r], jnp.zeros((EXT - RIM - width, channels), BF16)], axis=0
            )
    for i in range(rows):
        new_state[i] = jnp.concatenate([strip[i, 3 * RIM :], made[i, : width - LONREACH]], axis=0)
    for k in range(kcount):
        part = lax.dot_general(
            dext[...],
            weights[k * channels : (k + 1) * channels, :],
            (((1,), (1,)), ((), ())),
            preferred_element_type=F32,
        )
        part = part.astype(BF16).astype(F32)
        for c in range(chunks):
            dz[c, k * high * EXT : (k + 1) * high * EXT, :] = part[:, c * LANES : (c + 1) * LANES]
    for i in range(rows):
        for c in range(chunks):

            def add(n, acc):
                at = i * room + n
                return acc + val[at] * dz[c, pl.ds(pos[at], ROW), :]

            acc = lax.fori_loop(0, pos[rows * room + i], add, jnp.zeros((ROW, LANES), F32))
            lanes = slice(c * LANES, (c + 1) * LANES)
            adjoint = acc[:width].astype(BF16).astype(F32)
            state_grad[i, :, lanes] = (upstream[i, :, lanes].astype(F32) + adjoint).astype(BF16)


def backward(tables, weights, fields, made, upstream):
    rows, width, channels = upstream.shape
    high = rows + 2 * H
    kcount = weights.shape[0] // channels
    lists = rows * (high * tables[0].shape[0] + 1)
    block = jax.ShapeDtypeStruct((rows, width, channels), BF16)
    return pl.pallas_call(
        backward_kernel,
        out_shape=[block, block],
        in_specs=[SMEM] * 5 + [VMEM] * 7,
        out_specs=[VMEM] * 2,
        scratch_shapes=[
            pltpu.SMEM((lists + 8,), jnp.int32),
            pltpu.SMEM((lists,), F32),
            pltpu.VMEM((high * EXT, channels), BF16),
            pltpu.VMEM((channels // LANES, kcount * high * EXT, LANES), F32),
        ],
        compiler_params=pltpu.CompilerParams(vmem_limit_bytes=24 << 20),
        cost_estimate=pl.CostEstimate(flops=2_500_000_000, bytes_accessed=5_000_000, transcendentals=0),
    )(*tables, weights, *fields, made, upstream)


def lat_blocks(block):
    ends = lax.axis_size(LAT) - 1
    north = lax.ppermute(block, LAT, [(i, i + 1) for i in range(ends)])
    south = lax.ppermute(block, LAT, [(i + 1, i) for i in range(ends)])
    return north, south


def lon_shift(step):
    lons = lax.axis_size("lon")
    return [(j, (j + step) % lons) for j in range(lons)]


def lon_strips(side, rim):
    ends, lons = lax.axis_size(LAT) - 1, lax.axis_size("lon")
    along = lon_shift(-1)
    level = lax.ppermute(side, "lon", along)
    upper = lax.ppermute(rim, LAT + ("lon",), [(i * lons + c, (i + 1) * lons + d) for i in range(ends) for c, d in along])
    lower = lax.ppermute(rim, LAT + ("lon",), [((i + 1) * lons + c, i * lons + d) for i in range(ends) for c, d in along])
    return level, upper, lower


def core_swap(block):
    return lax.ppermute(block, "core", [(0, 1), (1, 0)])


def add_halves(keep, got, copies):
    def body(keep, got, out):
        rows = out.shape[1]
        total = (keep[...] + got[...].astype(F32)).astype(BF16)
        for n in range(copies):
            out[n] = total[n * rows : (n + 1) * rows]

    return pl.pallas_call(
        body,
        out_shape=jax.ShapeDtypeStruct((copies, keep.shape[0] // copies, keep.shape[1]), BF16),
        in_specs=[VMEM] * 2,
        out_specs=VMEM,
        compiler_params=pltpu.CompilerParams(vmem_limit_bytes=12 << 20),
    )(keep, got)


def join_halves(mine, other):
    def body(mine, other, out):
        half = mine.shape[0]
        first = lax.axis_index("core") == 0
        out[:half] = jnp.where(first, mine[...], other[...])
        out[half:] = jnp.where(first, other[...], mine[...])

    return pl.pallas_call(
        body,
        out_shape=jax.ShapeDtypeStruct((2 * mine.shape[0], mine.shape[1]), BF16),
        in_specs=[VMEM] * 2,
        out_specs=VMEM,
        compiler_params=pltpu.CompilerParams(vmem_limit_bytes=12 << 20),
    )(mine, other)


def sum_and_strip(pieces, copies, dmixed, north, south, made):
    def body(part, dmixed, north, south, made, out, strip):
        total = part[0]
        for n in range(1, part.shape[0]):
            total = total + part[n]
        total = total.astype(out.dtype)
        for n in range(copies):
            out[n] = total
        rows, width, _ = dmixed.shape
        for r in range(rows):
            for n, source in enumerate((north, south, dmixed)):
                strip[r, n * RIM : (n + 1) * RIM] = source[r, width - RIM :]
            strip[r, 3 * RIM :] = made[r, width - LONREACH :]

    rows, _, channels = dmixed.shape
    return pl.pallas_call(
        body,
        out_shape=[
            jax.ShapeDtypeStruct((copies, *pieces.shape[1:]), BF16),
            jax.ShapeDtypeStruct((rows, 3 * RIM + LONREACH, channels), BF16),
        ],
        in_specs=[VMEM] * 5,
        out_specs=[VMEM] * 2,
        compiler_params=pltpu.CompilerParams(vmem_limit_bytes=12 << 20),
    )(pieces, dmixed, north, south, made)


def sum_pieces(pieces, out_shape, passed=()):
    def body(*refs):
        part, out = refs[0], refs[1 + len(passed)]
        total = part[0].astype(F32)
        for n in range(1, part.shape[0]):
            total = total + part[n].astype(F32)
        total = total.astype(out.dtype)
        rows = out.shape[1]
        for n in range(out.shape[0]):
            out[n] = total if rows == total.shape[0] else total[n * rows : (n + 1) * rows]

    anywhere = pl.BlockSpec(memory_space=pl.ANY)
    return pl.pallas_call(
        body,
        out_shape=[out_shape] + [jax.ShapeDtypeStruct(x.shape, x.dtype) for x in passed],
        in_specs=[VMEM] + [anywhere] * len(passed),
        out_specs=[VMEM] + [anywhere] * len(passed),
        input_output_aliases={1 + n: 1 + n for n in range(len(passed))},
        compiler_params=pltpu.CompilerParams(vmem_limit_bytes=8 << 20),
    )(pieces, *passed)


def spread(block, copies, passed=()):
    def body(*refs):
        source, out = refs[0], refs[1 + len(passed)]
        for n in range(copies):
            out[n] = source[...]

    anywhere = pl.BlockSpec(memory_space=pl.ANY)
    return pl.pallas_call(
        body,
        out_shape=[jax.ShapeDtypeStruct((copies, *block.shape), block.dtype)]
        + [jax.ShapeDtypeStruct(x.shape, x.dtype) for x in passed],
        in_specs=[VMEM] + [anywhere] * len(passed),
        out_specs=[VMEM] + [anywhere] * len(passed),
        input_output_aliases={1 + n: 1 + n for n in range(len(passed))},
        compiler_params=pltpu.CompilerParams(vmem_limit_bytes=8 << 20),
    )(block, *passed)


def after(*arrays):
    def body(*refs):
        pass

    anywhere = pl.BlockSpec(memory_space=pl.ANY)
    return pl.pallas_call(
        body,
        out_shape=[jax.ShapeDtypeStruct(x.shape, x.dtype) for x in arrays],
        in_specs=[anywhere] * len(arrays),
        out_specs=[anywhere] * len(arrays),
        input_output_aliases={n: n for n in range(len(arrays))},
        compiler_params=pltpu.CompilerParams(vmem_limit_bytes=1 << 20),
    )(*arrays)


def exchange(pieces, axes):
    return lax.all_to_all(pieces, axes, 0, 0, tiled=True)


def shards(state, cotangent, weights, lat_off, lon_off, basis, tap_val, tap_count):
    field, upstream = state[0], cotangent[0]
    rows, width, channels = field.shape
    kcount = weights.shape[0]
    wide = weights.reshape(-1, channels)
    tables = (lat_off.T, lon_off.T, basis.T, tap_val.T, tap_count)
    side = jnp.concatenate([field[:, :RIM], upstream[:, :LONREACH]], axis=1)
    fields = (field, *lat_blocks(field), *lon_strips(side, field[:, :RIM]))
    cells = lax.axis_size(DP) * lax.axis_size(LAT) * rows * lax.axis_size("lon") * width
    nx, ny, nz = lax.axis_size(ALONG_X), lax.axis_size("y"), lax.axis_size("lon")
    made, dmixed, keep, send = forward(tables, wide, fields, upstream, 1.0 / math.sqrt(cells))
    piece = (keep.shape[0] // (nx * ny), channels)
    got = exchange(add_halves(keep, core_swap(send), nx), ALONG_X)
    part, dmixed = sum_pieces(got, jax.ShapeDtypeStruct((ny, *piece), BF16), (dmixed,))
    north, south = lat_blocks(dmixed)
    got = exchange(part, "y")
    (part,) = sum_pieces(got, jax.ShapeDtypeStruct((nz, *piece), F32))
    got = exchange(part, "lon")
    part, strip = sum_and_strip(got, ny, dmixed, north, south, made)
    strip = lax.ppermute(strip, "lon", lon_shift(1))
    got = exchange(part, "y")
    part, strip = spread(got.reshape(-1, channels), nx, (strip,))
    mine = exchange(part, ALONG_X).reshape(-1, channels)
    new_field, field_grad = backward(tables, wide, (dmixed, north, south, strip), made, upstream)
    mine, new_field, field_grad = after(mine, new_field, field_grad)
    weight_grad = join_halves(mine, core_swap(mine)).reshape(weights.shape)
    return new_field[None], field_grad[None], weight_grad


def solution(mesh):
    dp, lat, lon = (mesh.shape[name] for name in ("dp", "lat", "lon"))
    finer = jax.sharding.Mesh(mesh.devices.reshape(dp // 2, 2, lat // 2, 2, lon), DP + ("y", "x_lo", "lon"))
    cells = P(DP, LAT, "lon", None)
    return jax.shard_map(
        shards,
        mesh=finer,
        in_specs=(cells, cells, P(), P(), P(), P(), P(), P()),
        out_specs=(cells, cells, P()),
        check_vma=False,
    )
```

```python
import math

import jax
import jax.numpy as jnp
from jax import lax
from jax.experimental import pallas as pl
from jax.experimental.pallas import tpu as pltpu
from jax.sharding import PartitionSpec as P

H = 2
LONREACH = 24
RIM = 2 * LONREACH
LANES = 128
ROW = 192
EXT = ROW + RIM
SLOPE = math.sqrt(2.0 / math.pi)
CUBIC = 0.044715


SMEM = pl.BlockSpec(memory_space=pltpu.SMEM)
VMEM = pl.BlockSpec(memory_space=pltpu.VMEM)
BF16, F32 = jnp.bfloat16, jnp.float32
DP, LAT = ("x_hi", "core"), ("y", "x_lo")
ALONG_X = ("x_hi", "x_lo")


def forward_taps(tables, first, rows, kcount, pos, val):
    lat_off, lon_off, basis, tap_val, tap_count = tables
    taps = lat_off.shape[0]
    room = taps + 1
    for i in range(rows):
        row = first + i
        used = tap_count[row]
        counts = [jnp.int32(0) for _ in range(kcount)]
        for t in range(taps):
            where = (i + H + lat_off[t, row]) * EXT + LONREACH + lon_off[t, row]
            value = tap_val[t, row]
            kind = jnp.where(t < used, basis[t, row], kcount)
            for k in range(kcount):
                at = (i * kcount + k) * room + counts[k]
                pos[at] = where
                val[at] = value
                counts[k] = counts[k] + (kind == k).astype(jnp.int32)
        for k in range(kcount):
            pos[rows * kcount * room + i * kcount + k] = counts[k]


def backward_taps(tables, first, rows, pos, val):
    lat_off, lon_off, basis, tap_val, tap_count = tables
    taps, total = lat_off.shape
    high = rows + 2 * H
    room = high * taps + 1
    counts = [jnp.int32(0) for _ in range(rows)]
    for e in range(high):
        row = first + (e - H)
        inside = (row >= 0) & (row < total)
        row = jnp.clip(row, 0, total - 1)
        used = jnp.where(inside, tap_count[row], 0)
        for t in range(taps):
            where = (basis[t, row] * high + e) * EXT + LONREACH - lon_off[t, row]
            value = tap_val[t, row]
            target = jnp.where(t < used, e - H + lat_off[t, row], -1)
            for i in range(rows):
                at = i * room + counts[i]
                pos[at] = where
                val[at] = value
                counts[i] = counts[i] + (target == i).astype(jnp.int32)
    for i in range(rows):
        pos[rows * room + i] = counts[i]


def forward_kernel(lat_off, lon_off, basis, tap_val, tap_count, weights, own, north, south, east, ne, se, upstream,
                   new_state, dmixed, keep, send, pos, val, ext, up, z, dm, *, scale):
    rows, width, channels = own.shape
    kcount = weights.shape[0] // channels
    chunks = channels // LANES
    tables = (lat_off, lon_off, basis, tap_val, tap_count)
    room = lat_off.shape[0] + 1
    forward_taps(tables, lax.axis_index(LAT) * rows, rows, kcount, pos, val)
    for side, (mid, rim) in enumerate(((north, ne), (own, east), (south, se))):
        for r in range(rows):
            base = (side * rows + r) * EXT
            for c in range(chunks):
                lanes = slice(c * LANES, (c + 1) * LANES)
                ext[c, base : base + width, :] = mid[r, :, lanes].astype(F32)
                ext[c, base + width : base + width + RIM, :] = rim[r, :RIM, lanes].astype(F32)
                ext[c, base + width + RIM : base + EXT, :] = jnp.zeros((EXT - RIM - width, LANES), F32)
    for i in range(rows):
        kept = width - LONREACH
        up[i, :kept] = upstream[i].astype(F32)[LONREACH:]
        up[i, kept:width] = east[i].astype(F32)[RIM:]
    for i in range(rows):
        for k in range(kcount):
            for c in range(chunks):

                def add(n, acc):
                    at = (i * kcount + k) * room + n
                    return acc + val[at] * ext[c, pl.ds(pos[at], ROW), :]

                count = pos[rows * kcount * room + i * kcount + k]
                acc = lax.fori_loop(0, count, add, jnp.zeros((ROW, LANES), F32))
                col = k * channels + c * LANES
                z[i * ROW : (i + 1) * ROW, col : col + LANES] = acc.astype(BF16)
    mixed = jnp.dot(z[...], weights[...], preferred_element_type=F32)
    for i in range(rows):
        x = mixed[i * ROW : i * ROW + width]
        square = x * x
        t = jnp.tanh(SLOPE * (x + CUBIC * (square * x)))
        cdf = 0.5 * (1.0 + t)
        base = (H + i) * EXT + LONREACH
        field = jnp.concatenate([ext[c, base : base + width, :] for c in range(chunks)], axis=1)
        made = (field + x * cdf).astype(BF16)
        slope = cdf + x * (0.5 * (1.0 - t * t)) * (SLOPE * (1.0 + (3.0 * CUBIC) * square))
        d = (up[i, :width] * slope).astype(BF16)
        new_state[i] = made
        dmixed[i] = d
        dm[i * ROW : (i + 1) * ROW, :] = jnp.concatenate([d, jnp.zeros((ROW - width, channels), BF16)], axis=0)
    total = lax.dot_general(z[...], dm[...], (((0,), (0,)), ((), ())), preferred_element_type=F32)
    total = total * scale
    half = keep.shape[0]
    first = lax.axis_index("core") == 0
    keep[...] = jnp.where(first, total[:half], total[half:])
    send[...] = jnp.where(first, total[half:], total[:half]).astype(BF16)


def forward(tables, weights, fields, upstream, scale):
    rows, width, channels = upstream.shape
    wide = weights.shape[0]
    lists = rows * (wide // channels) * (tables[0].shape[0] + 1)
    block = jax.ShapeDtypeStruct((rows, width, channels), BF16)

    def body(*refs):
        forward_kernel(*refs, scale=scale)

    return pl.pallas_call(
        body,
        out_shape=[
            block,
            block,
            jax.ShapeDtypeStruct((wide // 2, channels), F32),
            jax.ShapeDtypeStruct((wide // 2, channels), BF16),
        ],
        in_specs=[SMEM] * 5 + [VMEM] * 8,
        out_specs=[VMEM] * 4,
        scratch_shapes=[
            pltpu.SMEM((lists + 64,), jnp.int32),
            pltpu.SMEM((lists,), F32),
            pltpu.VMEM((channels // LANES, (rows + 2 * H) * EXT, LANES), F32),
            pltpu.VMEM((rows, ROW, channels), F32),
            pltpu.VMEM((rows * ROW, wide), BF16),
            pltpu.VMEM((rows * ROW, channels), BF16),
        ],
        compiler_params=pltpu.CompilerParams(vmem_limit_bytes=24 << 20),
        cost_estimate=pl.CostEstimate(flops=2_000_000_000, bytes_accessed=8_000_000, transcendentals=140_000),
    )(*tables, weights, *fields, upstream)


def backward_kernel(lat_off, lon_off, basis, tap_val, tap_count, weights, own, north, south, strip, made, upstream,
                    new_state, state_grad, pos, val, dext, dz):
    rows, width, channels = own.shape
    kcount = weights.shape[0] // channels
    chunks = channels // LANES
    high = rows + 2 * H
    tables = (lat_off, lon_off, basis, tap_val, tap_count)
    room = high * lat_off.shape[0] + 1
    backward_taps(tables, lax.axis_index(LAT) * rows, rows, pos, val)
    for side, (mid, at) in enumerate(((north, 0), (own, 2 * RIM), (south, RIM))):
        for r in range(rows):
            base = (side * rows + r) * EXT
            dext[base : base + RIM, :] = strip[r, at : at + RIM]
            dext[base + RIM : base + EXT, :] = jnp.concatenate(
                [mid[r], jnp.zeros((EXT - RIM - width, channels), BF16)], axis=0
            )
    for i in range(rows):
        new_state[i] = jnp.concatenate([strip[i, 3 * RIM :], made[i, : width - LONREACH]], axis=0)
    for k in range(kcount):
        part = lax.dot_general(
            dext[...],
            weights[k * channels : (k + 1) * channels, :],
            (((1,), (1,)), ((), ())),
            preferred_element_type=F32,
        )
        part = part.astype(BF16).astype(F32)
        for c in range(chunks):
            dz[c, k * high * EXT : (k + 1) * high * EXT, :] = part[:, c * LANES : (c + 1) * LANES]
    for i in range(rows):
        for c in range(chunks):

            def add(n, acc):
                at = i * room + n
                return acc + val[at] * dz[c, pl.ds(pos[at], ROW), :]

            acc = lax.fori_loop(0, pos[rows * room + i], add, jnp.zeros((ROW, LANES), F32))
            lanes = slice(c * LANES, (c + 1) * LANES)
            adjoint = acc[:width].astype(BF16).astype(F32)
            state_grad[i, :, lanes] = (upstream[i, :, lanes].astype(F32) + adjoint).astype(BF16)


def backward(tables, weights, fields, made, upstream):
    rows, width, channels = upstream.shape
    high = rows + 2 * H
    kcount = weights.shape[0] // channels
    lists = rows * (high * tables[0].shape[0] + 1)
    block = jax.ShapeDtypeStruct((rows, width, channels), BF16)
    return pl.pallas_call(
        backward_kernel,
        out_shape=[block, block],
        in_specs=[SMEM] * 5 + [VMEM] * 7,
        out_specs=[VMEM] * 2,
        scratch_shapes=[
            pltpu.SMEM((lists + 8,), jnp.int32),
            pltpu.SMEM((lists,), F32),
            pltpu.VMEM((high * EXT, channels), BF16),
            pltpu.VMEM((channels // LANES, kcount * high * EXT, LANES), F32),
        ],
        compiler_params=pltpu.CompilerParams(vmem_limit_bytes=24 << 20),
        cost_estimate=pl.CostEstimate(flops=2_500_000_000, bytes_accessed=5_000_000, transcendentals=0),
    )(*tables, weights, *fields, made, upstream)


def from_north(block):
    return lax.ppermute(block, LAT, [(i, i + 1) for i in range(lax.axis_size(LAT) - 1)])


def from_south(block):
    return lax.ppermute(block, LAT, [(i + 1, i) for i in range(lax.axis_size(LAT) - 1)])


def lon_shift(step):
    lons = lax.axis_size("lon")
    return [(j, (j + step) % lons) for j in range(lons)]


def lon_strips(side, rim):
    ends, lons = lax.axis_size(LAT) - 1, lax.axis_size("lon")
    along = lon_shift(-1)
    level = lax.ppermute(side, "lon", along)
    upper = lax.ppermute(rim, LAT + ("lon",), [(i * lons + c, (i + 1) * lons + d) for i in range(ends) for c, d in along])
    lower = lax.ppermute(rim, LAT + ("lon",), [((i + 1) * lons + c, i * lons + d) for i in range(ends) for c, d in along])
    return level, upper, lower


def core_swap(block):
    return lax.ppermute(block, "core", [(0, 1), (1, 0)])


def add_halves(keep, got, copies):
    def body(keep, got, out):
        rows = out.shape[1]
        total = (keep[...] + got[...].astype(F32)).astype(BF16)
        for n in range(copies):
            out[n] = total[n * rows : (n + 1) * rows]

    return pl.pallas_call(
        body,
        out_shape=jax.ShapeDtypeStruct((copies, keep.shape[0] // copies, keep.shape[1]), BF16),
        in_specs=[VMEM] * 2,
        out_specs=VMEM,
        compiler_params=pltpu.CompilerParams(vmem_limit_bytes=12 << 20),
    )(keep, got)


def join_halves(mine, other):
    def body(mine, other, out):
        half = mine.shape[0]
        first = lax.axis_index("core") == 0
        out[:half] = jnp.where(first, mine[...], other[...])
        out[half:] = jnp.where(first, other[...], mine[...])

    return pl.pallas_call(
        body,
        out_shape=jax.ShapeDtypeStruct((2 * mine.shape[0], mine.shape[1]), BF16),
        in_specs=[VMEM] * 2,
        out_specs=VMEM,
        compiler_params=pltpu.CompilerParams(vmem_limit_bytes=12 << 20),
    )(mine, other)


def sum_and_strip(pieces, copies, dmixed, north, south, made):
    def body(part, dmixed, north, south, made, out, strip):
        total = part[0]
        for n in range(1, part.shape[0]):
            total = total + part[n]
        total = total.astype(out.dtype)
        for n in range(copies):
            out[n] = total
        rows, width, _ = dmixed.shape
        for r in range(rows):
            for n, source in enumerate((north, south, dmixed)):
                strip[r, n * RIM : (n + 1) * RIM] = source[r, width - RIM :]
            strip[r, 3 * RIM :] = made[r, width - LONREACH :]

    rows, _, channels = dmixed.shape
    return pl.pallas_call(
        body,
        out_shape=[
            jax.ShapeDtypeStruct((copies, *pieces.shape[1:]), BF16),
            jax.ShapeDtypeStruct((rows, 3 * RIM + LONREACH, channels), BF16),
        ],
        in_specs=[VMEM] * 5,
        out_specs=[VMEM] * 2,
        compiler_params=pltpu.CompilerParams(vmem_limit_bytes=12 << 20),
    )(pieces, dmixed, north, south, made)


def sum_pieces(pieces, out_shape, passed=()):
    def body(*refs):
        part, out = refs[0], refs[1 + len(passed)]
        total = part[0].astype(F32)
        for n in range(1, part.shape[0]):
            total = total + part[n].astype(F32)
        total = total.astype(out.dtype)
        rows = out.shape[1]
        for n in range(out.shape[0]):
            out[n] = total if rows == total.shape[0] else total[n * rows : (n + 1) * rows]

    anywhere = pl.BlockSpec(memory_space=pl.ANY)
    return pl.pallas_call(
        body,
        out_shape=[out_shape] + [jax.ShapeDtypeStruct(x.shape, x.dtype) for x in passed],
        in_specs=[VMEM] + [anywhere] * len(passed),
        out_specs=[VMEM] + [anywhere] * len(passed),
        input_output_aliases={1 + n: 1 + n for n in range(len(passed))},
        compiler_params=pltpu.CompilerParams(vmem_limit_bytes=8 << 20),
    )(pieces, *passed)


def spread(block, copies, passed=()):
    def body(*refs):
        source, out = refs[0], refs[1 + len(passed)]
        for n in range(copies):
            out[n] = source[...]

    anywhere = pl.BlockSpec(memory_space=pl.ANY)
    return pl.pallas_call(
        body,
        out_shape=[jax.ShapeDtypeStruct((copies, *block.shape), block.dtype)]
        + [jax.ShapeDtypeStruct(x.shape, x.dtype) for x in passed],
        in_specs=[VMEM] + [anywhere] * len(passed),
        out_specs=[VMEM] + [anywhere] * len(passed),
        input_output_aliases={1 + n: 1 + n for n in range(len(passed))},
        compiler_params=pltpu.CompilerParams(vmem_limit_bytes=8 << 20),
    )(block, *passed)


def after(*arrays):
    def body(*refs):
        pass

    anywhere = pl.BlockSpec(memory_space=pl.ANY)
    return pl.pallas_call(
        body,
        out_shape=[jax.ShapeDtypeStruct(x.shape, x.dtype) for x in arrays],
        in_specs=[anywhere] * len(arrays),
        out_specs=[anywhere] * len(arrays),
        input_output_aliases={n: n for n in range(len(arrays))},
        compiler_params=pltpu.CompilerParams(vmem_limit_bytes=1 << 20),
    )(*arrays)


def exchange(pieces, axes):
    return lax.all_to_all(pieces, axes, 0, 0, tiled=True)


def shards(state, cotangent, weights, lat_off, lon_off, basis, tap_val, tap_count):
    field, upstream = state[0], cotangent[0]
    rows, width, channels = field.shape
    kcount = weights.shape[0]
    wide = weights.reshape(-1, channels)
    tables = (lat_off.T, lon_off.T, basis.T, tap_val.T, tap_count)
    side = jnp.concatenate([field[:, :RIM], upstream[:, :LONREACH]], axis=1)
    fields = (field, from_north(field), from_south(field), *lon_strips(side, field[:, :RIM]))
    cells = lax.axis_size(DP) * lax.axis_size(LAT) * rows * lax.axis_size("lon") * width
    nx, ny, nz = lax.axis_size(ALONG_X), lax.axis_size("y"), lax.axis_size("lon")
    made, dmixed, keep, send = forward(tables, wide, fields, upstream, 1.0 / math.sqrt(cells))
    piece = (keep.shape[0] // (nx * ny), channels)
    got = exchange(add_halves(keep, core_swap(send), nx), ALONG_X)
    part, dmixed = sum_pieces(got, jax.ShapeDtypeStruct((ny, *piece), F32), (dmixed,))
    north = from_north(dmixed)
    got = exchange(part, "y")
    part, north, dmixed = sum_pieces(got, jax.ShapeDtypeStruct((nz, *piece), F32), (north, dmixed))
    south = from_south(dmixed)
    got = exchange(part, "lon")
    part, strip = sum_and_strip(got, ny, dmixed, north, south, made)
    strip = lax.ppermute(strip, "lon", lon_shift(1))
    got = exchange(part, "y")
    part, made = spread(got.reshape(-1, channels), nx, (made,))
    mine = exchange(part, ALONG_X).reshape(-1, channels)
    new_field, field_grad = backward(tables, wide, (dmixed, north, south, strip), made, upstream)
    mine, new_field, field_grad = after(mine, new_field, field_grad)
    weight_grad = join_halves(mine, core_swap(mine)).reshape(weights.shape)
    return new_field[None], field_grad[None], weight_grad


def solution(mesh):
    dp, lat, lon = (mesh.shape[name] for name in ("dp", "lat", "lon"))
    finer = jax.sharding.Mesh(mesh.devices.reshape(dp // 2, 2, lat // 2, 2, lon), DP + ("y", "x_lo", "lon"))
    cells = P(DP, LAT, "lon", None)
    return jax.shard_map(
        shards,
        mesh=finer,
        in_specs=(cells, cells, P(), P(), P(), P(), P(), P()),
        out_specs=(cells, cells, P()),
        check_vma=False,
    )
```

```python
import math

import jax
import jax.numpy as jnp
from jax import lax
from jax.experimental import pallas as pl
from jax.experimental.pallas import tpu as pltpu
from jax.sharding import PartitionSpec as P

H = 2
LONREACH = 24
RIM = 2 * LONREACH
LANES = 128
ROW = 192
EXT = ROW + RIM
SLOPE = math.sqrt(2.0 / math.pi)
CUBIC = 0.044715


SMEM = pl.BlockSpec(memory_space=pltpu.SMEM)
VMEM = pl.BlockSpec(memory_space=pltpu.VMEM)
BF16, F32 = jnp.bfloat16, jnp.float32
DP, LAT = ("x_hi", "core"), ("y", "x_lo")
ALONG_X = ("x_hi", "x_lo")


def forward_taps(tables, first, rows, kcount, pos, val):
    lat_off, lon_off, basis, tap_val, tap_count = tables
    taps = lat_off.shape[0]
    room = taps + 1
    for i in range(rows):
        row = first + i
        used = tap_count[row]
        counts = [jnp.int32(0) for _ in range(kcount)]
        for t in range(taps):
            where = (i + H + lat_off[t, row]) * EXT + LONREACH + lon_off[t, row]
            value = tap_val[t, row]
            kind = jnp.where(t < used, basis[t, row], kcount)
            for k in range(kcount):
                at = (i * kcount + k) * room + counts[k]
                pos[at] = where
                val[at] = value
                counts[k] = counts[k] + (kind == k).astype(jnp.int32)
        for k in range(kcount):
            pos[rows * kcount * room + i * kcount + k] = counts[k]


def backward_taps(tables, first, rows, pos, val):
    lat_off, lon_off, basis, tap_val, tap_count = tables
    taps, total = lat_off.shape
    high = rows + 2 * H
    room = high * taps + 1
    counts = [jnp.int32(0) for _ in range(rows)]
    for e in range(high):
        row = first + (e - H)
        inside = (row >= 0) & (row < total)
        row = jnp.clip(row, 0, total - 1)
        used = jnp.where(inside, tap_count[row], 0)
        for t in range(taps):
            where = (basis[t, row] * high + e) * EXT + LONREACH - lon_off[t, row]
            value = tap_val[t, row]
            target = jnp.where(t < used, e - H + lat_off[t, row], -1)
            for i in range(rows):
                at = i * room + counts[i]
                pos[at] = where
                val[at] = value
                counts[i] = counts[i] + (target == i).astype(jnp.int32)
    for i in range(rows):
        pos[rows * room + i] = counts[i]


def forward_kernel(lat_off, lon_off, basis, tap_val, tap_count, weights, own, north, south, east, ne, se, upstream,
                   new_state, dmixed, keep, send, pos, val, ext, up, z, dm, *, scale):
    rows, width, channels = own.shape
    kcount = weights.shape[0] // channels
    chunks = channels // LANES
    tables = (lat_off, lon_off, basis, tap_val, tap_count)
    room = lat_off.shape[0] + 1
    forward_taps(tables, lax.axis_index(LAT) * rows, rows, kcount, pos, val)
    for side, (mid, rim) in enumerate(((north, ne), (own, east), (south, se))):
        for r in range(rows):
            base = (side * rows + r) * EXT
            for c in range(chunks):
                lanes = slice(c * LANES, (c + 1) * LANES)
                ext[c, base : base + width, :] = mid[r, :, lanes].astype(F32)
                ext[c, base + width : base + width + RIM, :] = rim[r, :RIM, lanes].astype(F32)
                ext[c, base + width + RIM : base + EXT, :] = jnp.zeros((EXT - RIM - width, LANES), F32)
    for i in range(rows):
        kept = width - LONREACH
        up[i, :kept] = upstream[i].astype(F32)[LONREACH:]
        up[i, kept:width] = east[i].astype(F32)[RIM:]
    for i in range(rows):
        for k in range(kcount):
            for c in range(chunks):

                def add(n, acc):
                    at = (i * kcount + k) * room + n
                    return acc + val[at] * ext[c, pl.ds(pos[at], ROW), :]

                count = pos[rows * kcount * room + i * kcount + k]
                acc = lax.fori_loop(0, count, add, jnp.zeros((ROW, LANES), F32))
                col = k * channels + c * LANES
                z[i * ROW : (i + 1) * ROW, col : col + LANES] = acc.astype(BF16)
    mixed = jnp.dot(z[...], weights[...], preferred_element_type=F32)
    for i in range(rows):
        x = mixed[i * ROW : i * ROW + width]
        square = x * x
        t = jnp.tanh(SLOPE * (x + CUBIC * (square * x)))
        cdf = 0.5 * (1.0 + t)
        base = (H + i) * EXT + LONREACH
        field = jnp.concatenate([ext[c, base : base + width, :] for c in range(chunks)], axis=1)
        made = (field + x * cdf).astype(BF16)
        slope = cdf + x * (0.5 * (1.0 - t * t)) * (SLOPE * (1.0 + (3.0 * CUBIC) * square))
        d = (up[i, :width] * slope).astype(BF16)
        new_state[i] = made
        dmixed[i] = d
        dm[i * ROW : (i + 1) * ROW, :] = jnp.concatenate([d, jnp.zeros((ROW - width, channels), BF16)], axis=0)
    total = lax.dot_general(z[...], dm[...], (((0,), (0,)), ((), ())), preferred_element_type=F32)
    total = total * scale
    half = keep.shape[0]
    first = lax.axis_index("core") == 0
    keep[...] = jnp.where(first, total[:half], total[half:])
    send[...] = jnp.where(first, total[half:], total[:half]).astype(BF16)


def forward(tables, weights, fields, upstream, scale):
    rows, width, channels = upstream.shape
    wide = weights.shape[0]
    lists = rows * (wide // channels) * (tables[0].shape[0] + 1)
    block = jax.ShapeDtypeStruct((rows, width, channels), BF16)

    def body(*refs):
        forward_kernel(*refs, scale=scale)

    return pl.pallas_call(
        body,
        out_shape=[
            block,
            block,
            jax.ShapeDtypeStruct((wide // 2, channels), F32),
            jax.ShapeDtypeStruct((wide // 2, channels), BF16),
        ],
        in_specs=[SMEM] * 5 + [VMEM] * 8,
        out_specs=[VMEM] * 4,
        scratch_shapes=[
            pltpu.SMEM((lists + 64,), jnp.int32),
            pltpu.SMEM((lists,), F32),
            pltpu.VMEM((channels // LANES, (rows + 2 * H) * EXT, LANES), F32),
            pltpu.VMEM((rows, ROW, channels), F32),
            pltpu.VMEM((rows * ROW, wide), BF16),
            pltpu.VMEM((rows * ROW, channels), BF16),
        ],
        compiler_params=pltpu.CompilerParams(vmem_limit_bytes=24 << 20),
        cost_estimate=pl.CostEstimate(flops=2_000_000_000, bytes_accessed=8_000_000, transcendentals=140_000),
    )(*tables, weights, *fields, upstream)


def backward_kernel(lat_off, lon_off, basis, tap_val, tap_count, weights, own, north, south, strip, made, upstream,
                    new_state, state_grad, pos, val, dext, dz):
    rows, width, channels = own.shape
    kcount = weights.shape[0] // channels
    chunks = channels // LANES
    high = rows + 2 * H
    tables = (lat_off, lon_off, basis, tap_val, tap_count)
    room = high * lat_off.shape[0] + 1
    backward_taps(tables, lax.axis_index(LAT) * rows, rows, pos, val)
    for side, (mid, at) in enumerate(((north, 0), (own, 2 * RIM), (south, RIM))):
        for r in range(rows):
            base = (side * rows + r) * EXT
            dext[base : base + RIM, :] = strip[r, at : at + RIM]
            dext[base + RIM : base + EXT, :] = jnp.concatenate(
                [mid[r], jnp.zeros((EXT - RIM - width, channels), BF16)], axis=0
            )
    for i in range(rows):
        new_state[i] = jnp.concatenate([strip[i, 3 * RIM :], made[i, : width - LONREACH]], axis=0)
    for k in range(kcount):
        part = lax.dot_general(
            dext[...],
            weights[k * channels : (k + 1) * channels, :],
            (((1,), (1,)), ((), ())),
            preferred_element_type=F32,
        )
        part = part.astype(BF16).astype(F32)
        for c in range(chunks):
            dz[c, k * high * EXT : (k + 1) * high * EXT, :] = part[:, c * LANES : (c + 1) * LANES]
    for i in range(rows):
        for c in range(chunks):

            def add(n, acc):
                at = i * room + n
                return acc + val[at] * dz[c, pl.ds(pos[at], ROW), :]

            acc = lax.fori_loop(0, pos[rows * room + i], add, jnp.zeros((ROW, LANES), F32))
            lanes = slice(c * LANES, (c + 1) * LANES)
            adjoint = acc[:width].astype(BF16).astype(F32)
            state_grad[i, :, lanes] = (upstream[i, :, lanes].astype(F32) + adjoint).astype(BF16)


def backward(tables, weights, fields, made, upstream):
    rows, width, channels = upstream.shape
    high = rows + 2 * H
    kcount = weights.shape[0] // channels
    lists = rows * (high * tables[0].shape[0] + 1)
    block = jax.ShapeDtypeStruct((rows, width, channels), BF16)
    return pl.pallas_call(
        backward_kernel,
        out_shape=[block, block],
        in_specs=[SMEM] * 5 + [VMEM] * 7,
        out_specs=[VMEM] * 2,
        scratch_shapes=[
            pltpu.SMEM((lists + 8,), jnp.int32),
            pltpu.SMEM((lists,), F32),
            pltpu.VMEM((high * EXT, channels), BF16),
            pltpu.VMEM((channels // LANES, kcount * high * EXT, LANES), F32),
        ],
        compiler_params=pltpu.CompilerParams(vmem_limit_bytes=24 << 20),
        cost_estimate=pl.CostEstimate(flops=2_500_000_000, bytes_accessed=5_000_000, transcendentals=0),
    )(*tables, weights, *fields, made, upstream)


def from_north(block):
    return lax.ppermute(block, LAT, [(i, i + 1) for i in range(lax.axis_size(LAT) - 1)])


def from_south(block):
    return lax.ppermute(block, LAT, [(i + 1, i) for i in range(lax.axis_size(LAT) - 1)])


def lon_shift(step):
    lons = lax.axis_size("lon")
    return [(j, (j + step) % lons) for j in range(lons)]


def lon_strips(side, rim):
    ends, lons = lax.axis_size(LAT) - 1, lax.axis_size("lon")
    along = lon_shift(-1)
    level = lax.ppermute(side, "lon", along)
    upper = lax.ppermute(rim, LAT + ("lon",), [(i * lons + c, (i + 1) * lons + d) for i in range(ends) for c, d in along])
    lower = lax.ppermute(rim, LAT + ("lon",), [((i + 1) * lons + c, i * lons + d) for i in range(ends) for c, d in along])
    return level, upper, lower


def core_swap(block):
    return lax.ppermute(block, "core", [(0, 1), (1, 0)])


def add_halves(keep, got, copies):
    def body(keep, got, out):
        rows = out.shape[1]
        total = (keep[...] + got[...].astype(F32)).astype(BF16)
        for n in range(copies):
            out[n] = total[n * rows : (n + 1) * rows]

    return pl.pallas_call(
        body,
        out_shape=jax.ShapeDtypeStruct((copies, keep.shape[0] // copies, keep.shape[1]), BF16),
        in_specs=[VMEM] * 2,
        out_specs=VMEM,
        compiler_params=pltpu.CompilerParams(vmem_limit_bytes=12 << 20),
    )(keep, got)


def join_halves(mine, other):
    def body(mine, other, out):
        half = mine.shape[0]
        first = lax.axis_index("core") == 0
        out[:half] = jnp.where(first, mine[...], other[...])
        out[half:] = jnp.where(first, other[...], mine[...])

    return pl.pallas_call(
        body,
        out_shape=jax.ShapeDtypeStruct((2 * mine.shape[0], mine.shape[1]), BF16),
        in_specs=[VMEM] * 2,
        out_specs=VMEM,
        compiler_params=pltpu.CompilerParams(vmem_limit_bytes=12 << 20),
    )(mine, other)


def strip_for_east(dmixed, north, south, made):
    def body(dmixed, north, south, made, strip):
        rows, width, _ = dmixed.shape
        for r in range(rows):
            for n, source in enumerate((north, south, dmixed)):
                strip[r, n * RIM : (n + 1) * RIM] = source[r, width - RIM :]
            strip[r, 3 * RIM :] = made[r, width - LONREACH :]

    rows, _, channels = dmixed.shape
    return pl.pallas_call(
        body,
        out_shape=jax.ShapeDtypeStruct((rows, 3 * RIM + LONREACH, channels), BF16),
        in_specs=[VMEM] * 4,
        out_specs=VMEM,
        compiler_params=pltpu.CompilerParams(vmem_limit_bytes=8 << 20),
    )(dmixed, north, south, made)


def sum_pieces(pieces, out_shape, passed=()):
    def body(*refs):
        part, out = refs[0], refs[1 + len(passed)]
        total = part[0].astype(F32)
        for n in range(1, part.shape[0]):
            total = total + part[n].astype(F32)
        total = total.astype(out.dtype)
        rows = out.shape[1]
        for n in range(out.shape[0]):
            out[n] = total if rows == total.shape[0] else total[n * rows : (n + 1) * rows]

    anywhere = pl.BlockSpec(memory_space=pl.ANY)
    return pl.pallas_call(
        body,
        out_shape=[out_shape] + [jax.ShapeDtypeStruct(x.shape, x.dtype) for x in passed],
        in_specs=[VMEM] + [anywhere] * len(passed),
        out_specs=[VMEM] + [anywhere] * len(passed),
        input_output_aliases={1 + n: 1 + n for n in range(len(passed))},
        compiler_params=pltpu.CompilerParams(vmem_limit_bytes=8 << 20),
    )(pieces, *passed)


def spread(block, copies, passed=()):
    def body(*refs):
        source, out = refs[0], refs[1 + len(passed)]
        for n in range(copies):
            out[n] = source[...]

    anywhere = pl.BlockSpec(memory_space=pl.ANY)
    return pl.pallas_call(
        body,
        out_shape=[jax.ShapeDtypeStruct((copies, *block.shape), block.dtype)]
        + [jax.ShapeDtypeStruct(x.shape, x.dtype) for x in passed],
        in_specs=[VMEM] + [anywhere] * len(passed),
        out_specs=[VMEM] + [anywhere] * len(passed),
        input_output_aliases={1 + n: 1 + n for n in range(len(passed))},
        compiler_params=pltpu.CompilerParams(vmem_limit_bytes=8 << 20),
    )(block, *passed)


def after(*arrays):
    def body(*refs):
        pass

    anywhere = pl.BlockSpec(memory_space=pl.ANY)
    return pl.pallas_call(
        body,
        out_shape=[jax.ShapeDtypeStruct(x.shape, x.dtype) for x in arrays],
        in_specs=[anywhere] * len(arrays),
        out_specs=[anywhere] * len(arrays),
        input_output_aliases={n: n for n in range(len(arrays))},
        compiler_params=pltpu.CompilerParams(vmem_limit_bytes=1 << 20),
    )(*arrays)


def exchange(pieces, axes):
    return lax.all_to_all(pieces, axes, 0, 0, tiled=True)


def shards(state, cotangent, weights, lat_off, lon_off, basis, tap_val, tap_count):
    field, upstream = state[0], cotangent[0]
    rows, width, channels = field.shape
    kcount = weights.shape[0]
    wide = weights.reshape(-1, channels)
    tables = (lat_off.T, lon_off.T, basis.T, tap_val.T, tap_count)
    side = jnp.concatenate([field[:, :RIM], upstream[:, :LONREACH]], axis=1)
    fields = (field, from_north(field), from_south(field), *lon_strips(side, field[:, :RIM]))
    cells = lax.axis_size(DP) * lax.axis_size(LAT) * rows * lax.axis_size("lon") * width
    nx, ny, nz = lax.axis_size(ALONG_X), lax.axis_size("y"), lax.axis_size("lon")
    made, dmixed, keep, send = forward(tables, wide, fields, upstream, 1.0 / math.sqrt(cells))
    piece = (keep.shape[0] // (nx * ny), channels)
    got = exchange(add_halves(keep, core_swap(send), nx * ny), ALONG_X + ("y",))
    north, south = from_north(dmixed), from_south(dmixed)
    part, north, south = sum_pieces(got, jax.ShapeDtypeStruct((nz, *piece), F32), (north, south))
    got = exchange(part, "lon")
    part, dmixed = sum_pieces(got, jax.ShapeDtypeStruct((ny, *piece), BF16), (dmixed,))
    strip = lax.ppermute(strip_for_east(dmixed, north, south, made), "lon", lon_shift(1))
    got = exchange(part, "y")
    part, made = spread(got.reshape(-1, channels), nx, (made,))
    mine = exchange(part, ALONG_X).reshape(-1, channels)
    new_field, field_grad = backward(tables, wide, (dmixed, north, south, strip), made, upstream)
    mine, new_field, field_grad = after(mine, new_field, field_grad)
    weight_grad = join_halves(mine, core_swap(mine)).reshape(weights.shape)
    return new_field[None], field_grad[None], weight_grad


def solution(mesh):
    dp, lat, lon = (mesh.shape[name] for name in ("dp", "lat", "lon"))
    finer = jax.sharding.Mesh(mesh.devices.reshape(dp // 2, 2, lat // 2, 2, lon), DP + ("y", "x_lo", "lon"))
    cells = P(DP, LAT, "lon", None)
    return jax.shard_map(
        shards,
        mesh=finer,
        in_specs=(cells, cells, P(), P(), P(), P(), P(), P()),
        out_specs=(cells, cells, P()),
        check_vma=False,
    )
```

```python
import math

import jax
import jax.numpy as jnp
from jax import lax
from jax.experimental import pallas as pl
from jax.experimental.pallas import tpu as pltpu
from jax.sharding import PartitionSpec as P

H = 2
LONREACH = 24
RIM = 2 * LONREACH
LANES = 128
ROW = 192
EXT = ROW + RIM
SLOPE = math.sqrt(2.0 / math.pi)
CUBIC = 0.044715


SMEM = pl.BlockSpec(memory_space=pltpu.SMEM)
VMEM = pl.BlockSpec(memory_space=pltpu.VMEM)
BF16, F32 = jnp.bfloat16, jnp.float32
DP, LAT = ("x_hi", "core"), ("y", "x_lo")
ALONG_X = ("x_hi", "x_lo")


def forward_taps(tables, first, rows, kcount, pos, val):
    lat_off, lon_off, basis, tap_val, tap_count = tables
    taps = lat_off.shape[0]
    room = taps + 1
    for i in range(rows):
        row = first + i
        used = tap_count[row]
        counts = [jnp.int32(0) for _ in range(kcount)]
        for t in range(taps):
            where = (i + H + lat_off[t, row]) * EXT + LONREACH + lon_off[t, row]
            value = tap_val[t, row]
            kind = jnp.where(t < used, basis[t, row], kcount)
            for k in range(kcount):
                at = (i * kcount + k) * room + counts[k]
                pos[at] = where
                val[at] = value
                counts[k] = counts[k] + (kind == k).astype(jnp.int32)
        for k in range(kcount):
            pos[rows * kcount * room + i * kcount + k] = counts[k]


def backward_taps(tables, first, rows, pos, val):
    lat_off, lon_off, basis, tap_val, tap_count = tables
    taps, total = lat_off.shape
    high = rows + 2 * H
    room = high * taps + 1
    counts = [jnp.int32(0) for _ in range(rows)]
    for e in range(high):
        row = first + (e - H)
        inside = (row >= 0) & (row < total)
        row = jnp.clip(row, 0, total - 1)
        used = jnp.where(inside, tap_count[row], 0)
        for t in range(taps):
            where = (basis[t, row] * high + e) * EXT + LONREACH - lon_off[t, row]
            value = tap_val[t, row]
            target = jnp.where(t < used, e - H + lat_off[t, row], -1)
            for i in range(rows):
                at = i * room + counts[i]
                pos[at] = where
                val[at] = value
                counts[i] = counts[i] + (target == i).astype(jnp.int32)
    for i in range(rows):
        pos[rows * room + i] = counts[i]


def forward_kernel(lat_off, lon_off, basis, tap_val, tap_count, weights, own, north, south, strip, upstream,
                   new_state, dmixed, keep, send, pos, val, ext, up, z, dm, *, scale):
    rows, width, channels = own.shape
    kcount = weights.shape[0] // channels
    chunks = channels // LANES
    tables = (lat_off, lon_off, basis, tap_val, tap_count)
    room = lat_off.shape[0] + 1
    forward_taps(tables, lax.axis_index(LAT) * rows, rows, kcount, pos, val)
    for side, (mid, at) in enumerate(((north, 0), (own, 2 * RIM), (south, RIM))):
        for r in range(rows):
            base = (side * rows + r) * EXT
            for c in range(chunks):
                lanes = slice(c * LANES, (c + 1) * LANES)
                ext[c, base : base + width, :] = mid[r, :, lanes].astype(F32)
                ext[c, base + width : base + width + RIM, :] = strip[r, at : at + RIM, lanes].astype(F32)
                ext[c, base + width + RIM : base + EXT, :] = jnp.zeros((EXT - RIM - width, LANES), F32)
    for i in range(rows):
        kept = width - LONREACH
        up[i, :kept] = upstream[i].astype(F32)[LONREACH:]
        up[i, kept:width] = strip[i].astype(F32)[3 * RIM :]
    for i in range(rows):
        for k in range(kcount):
            for c in range(chunks):

                def add(n, acc):
                    at = (i * kcount + k) * room + n
                    return acc + val[at] * ext[c, pl.ds(pos[at], ROW), :]

                count = pos[rows * kcount * room + i * kcount + k]
                acc = lax.fori_loop(0, count, add, jnp.zeros((ROW, LANES), F32))
                col = k * channels + c * LANES
                z[i * ROW : (i + 1) * ROW, col : col + LANES] = acc.astype(BF16)
    mixed = jnp.dot(z[...], weights[...], preferred_element_type=F32)
    for i in range(rows):
        x = mixed[i * ROW : i * ROW + width]
        square = x * x
        t = jnp.tanh(SLOPE * (x + CUBIC * (square * x)))
        cdf = 0.5 * (1.0 + t)
        base = (H + i) * EXT + LONREACH
        field = jnp.concatenate([ext[c, base : base + width, :] for c in range(chunks)], axis=1)
        made = (field + x * cdf).astype(BF16)
        slope = cdf + x * (0.5 * (1.0 - t * t)) * (SLOPE * (1.0 + (3.0 * CUBIC) * square))
        d = (up[i, :width] * slope).astype(BF16)
        new_state[i] = made
        dmixed[i] = d
        dm[i * ROW : (i + 1) * ROW, :] = jnp.concatenate([d, jnp.zeros((ROW - width, channels), BF16)], axis=0)
    total = lax.dot_general(z[...], dm[...], (((0,), (0,)), ((), ())), preferred_element_type=F32)
    total = total * scale
    half = keep.shape[0]
    first = lax.axis_index("core") == 0
    keep[...] = jnp.where(first, total[:half], total[half:])
    send[...] = jnp.where(first, total[half:], total[:half]).astype(BF16)


def forward(tables, weights, fields, upstream, scale):
    rows, width, channels = upstream.shape
    wide = weights.shape[0]
    lists = rows * (wide // channels) * (tables[0].shape[0] + 1)
    block = jax.ShapeDtypeStruct((rows, width, channels), BF16)

    def body(*refs):
        forward_kernel(*refs, scale=scale)

    return pl.pallas_call(
        body,
        out_shape=[
            block,
            block,
            jax.ShapeDtypeStruct((wide // 2, channels), F32),
            jax.ShapeDtypeStruct((wide // 2, channels), BF16),
        ],
        in_specs=[SMEM] * 5 + [VMEM] * 6,
        out_specs=[VMEM] * 4,
        scratch_shapes=[
            pltpu.SMEM((lists + 64,), jnp.int32),
            pltpu.SMEM((lists,), F32),
            pltpu.VMEM((channels // LANES, (rows + 2 * H) * EXT, LANES), F32),
            pltpu.VMEM((rows, ROW, channels), F32),
            pltpu.VMEM((rows * ROW, wide), BF16),
            pltpu.VMEM((rows * ROW, channels), BF16),
        ],
        compiler_params=pltpu.CompilerParams(vmem_limit_bytes=24 << 20),
        cost_estimate=pl.CostEstimate(flops=2_000_000_000, bytes_accessed=8_000_000, transcendentals=140_000),
    )(*tables, weights, *fields, upstream)


def backward_kernel(lat_off, lon_off, basis, tap_val, tap_count, weights, own, north, south, strip, made, upstream,
                    new_state, state_grad, pos, val, dext, dz):
    rows, width, channels = own.shape
    kcount = weights.shape[0] // channels
    chunks = channels // LANES
    high = rows + 2 * H
    tables = (lat_off, lon_off, basis, tap_val, tap_count)
    room = high * lat_off.shape[0] + 1
    backward_taps(tables, lax.axis_index(LAT) * rows, rows, pos, val)
    for side, (mid, at) in enumerate(((north, 0), (own, 2 * RIM), (south, RIM))):
        for r in range(rows):
            base = (side * rows + r) * EXT
            dext[base : base + RIM, :] = strip[r, at : at + RIM]
            dext[base + RIM : base + EXT, :] = jnp.concatenate(
                [mid[r], jnp.zeros((EXT - RIM - width, channels), BF16)], axis=0
            )
    for i in range(rows):
        new_state[i] = jnp.concatenate([strip[i, 3 * RIM :], made[i, : width - LONREACH]], axis=0)
    for k in range(kcount):
        part = lax.dot_general(
            dext[...],
            weights[k * channels : (k + 1) * channels, :],
            (((1,), (1,)), ((), ())),
            preferred_element_type=F32,
        )
        part = part.astype(BF16).astype(F32)
        for c in range(chunks):
            dz[c, k * high * EXT : (k + 1) * high * EXT, :] = part[:, c * LANES : (c + 1) * LANES]
    for i in range(rows):
        for c in range(chunks):

            def add(n, acc):
                at = i * room + n
                return acc + val[at] * dz[c, pl.ds(pos[at], ROW), :]

            acc = lax.fori_loop(0, pos[rows * room + i], add, jnp.zeros((ROW, LANES), F32))
            lanes = slice(c * LANES, (c + 1) * LANES)
            adjoint = acc[:width].astype(BF16).astype(F32)
            state_grad[i, :, lanes] = (upstream[i, :, lanes].astype(F32) + adjoint).astype(BF16)


def backward(tables, weights, fields, made, upstream):
    rows, width, channels = upstream.shape
    high = rows + 2 * H
    kcount = weights.shape[0] // channels
    lists = rows * (high * tables[0].shape[0] + 1)
    block = jax.ShapeDtypeStruct((rows, width, channels), BF16)
    return pl.pallas_call(
        backward_kernel,
        out_shape=[block, block],
        in_specs=[SMEM] * 5 + [VMEM] * 7,
        out_specs=[VMEM] * 2,
        scratch_shapes=[
            pltpu.SMEM((lists + 8,), jnp.int32),
            pltpu.SMEM((lists,), F32),
            pltpu.VMEM((high * EXT, channels), BF16),
            pltpu.VMEM((channels // LANES, kcount * high * EXT, LANES), F32),
        ],
        compiler_params=pltpu.CompilerParams(vmem_limit_bytes=24 << 20),
        cost_estimate=pl.CostEstimate(flops=2_500_000_000, bytes_accessed=5_000_000, transcendentals=0),
    )(*tables, weights, *fields, made, upstream)


def lat_blocks(block):
    ends = lax.axis_size(LAT) - 1
    north = lax.ppermute(block, LAT, [(i, i + 1) for i in range(ends)])
    south = lax.ppermute(block, LAT, [(i + 1, i) for i in range(ends)])
    return north, south


def lon_shift(step):
    lons = lax.axis_size("lon")
    return [(j, (j + step) % lons) for j in range(lons)]


def strip_for_west(field, north, south, upstream):
    def body(field, north, south, upstream, strip):
        for r in range(field.shape[0]):
            for n, source in enumerate((north, south, field)):
                strip[r, n * RIM : (n + 1) * RIM] = source[r, :RIM]
            strip[r, 3 * RIM :] = upstream[r, :LONREACH]

    rows, _, channels = field.shape
    return pl.pallas_call(
        body,
        out_shape=jax.ShapeDtypeStruct((rows, 3 * RIM + LONREACH, channels), BF16),
        in_specs=[VMEM] * 4,
        out_specs=VMEM,
        compiler_params=pltpu.CompilerParams(vmem_limit_bytes=8 << 20),
    )(field, north, south, upstream)


def core_swap(block):
    return lax.ppermute(block, "core", [(0, 1), (1, 0)])


def add_halves(keep, got, copies):
    def body(keep, got, out):
        rows = out.shape[1]
        total = (keep[...] + got[...].astype(F32)).astype(BF16)
        for n in range(copies):
            out[n] = total[n * rows : (n + 1) * rows]

    return pl.pallas_call(
        body,
        out_shape=jax.ShapeDtypeStruct((copies, keep.shape[0] // copies, keep.shape[1]), BF16),
        in_specs=[VMEM] * 2,
        out_specs=VMEM,
        compiler_params=pltpu.CompilerParams(vmem_limit_bytes=12 << 20),
    )(keep, got)


def join_halves(mine, other):
    def body(mine, other, out):
        half = mine.shape[0]
        first = lax.axis_index("core") == 0
        out[:half] = jnp.where(first, mine[...], other[...])
        out[half:] = jnp.where(first, other[...], mine[...])

    return pl.pallas_call(
        body,
        out_shape=jax.ShapeDtypeStruct((2 * mine.shape[0], mine.shape[1]), BF16),
        in_specs=[VMEM] * 2,
        out_specs=VMEM,
        compiler_params=pltpu.CompilerParams(vmem_limit_bytes=12 << 20),
    )(mine, other)


def sum_and_strip(pieces, copies, dmixed, north, south, made):
    def body(part, dmixed, north, south, made, out, strip):
        total = part[0]
        for n in range(1, part.shape[0]):
            total = total + part[n]
        total = total.astype(out.dtype)
        for n in range(copies):
            out[n] = total
        rows, width, _ = dmixed.shape
        for r in range(rows):
            for n, source in enumerate((north, south, dmixed)):
                strip[r, n * RIM : (n + 1) * RIM] = source[r, width - RIM :]
            strip[r, 3 * RIM :] = made[r, width - LONREACH :]

    rows, _, channels = dmixed.shape
    return pl.pallas_call(
        body,
        out_shape=[
            jax.ShapeDtypeStruct((copies, *pieces.shape[1:]), BF16),
            jax.ShapeDtypeStruct((rows, 3 * RIM + LONREACH, channels), BF16),
        ],
        in_specs=[VMEM] * 5,
        out_specs=[VMEM] * 2,
        compiler_params=pltpu.CompilerParams(vmem_limit_bytes=12 << 20),
    )(pieces, dmixed, north, south, made)


def sum_pieces(pieces, out_shape, passed=()):
    def body(*refs):
        part, out = refs[0], refs[1 + len(passed)]
        total = part[0].astype(F32)
        for n in range(1, part.shape[0]):
            total = total + part[n].astype(F32)
        total = total.astype(out.dtype)
        rows = out.shape[1]
        for n in range(out.shape[0]):
            out[n] = total if rows == total.shape[0] else total[n * rows : (n + 1) * rows]

    anywhere = pl.BlockSpec(memory_space=pl.ANY)
    return pl.pallas_call(
        body,
        out_shape=[out_shape] + [jax.ShapeDtypeStruct(x.shape, x.dtype) for x in passed],
        in_specs=[VMEM] + [anywhere] * len(passed),
        out_specs=[VMEM] + [anywhere] * len(passed),
        input_output_aliases={1 + n: 1 + n for n in range(len(passed))},
        compiler_params=pltpu.CompilerParams(vmem_limit_bytes=8 << 20),
    )(pieces, *passed)


def spread(block, copies, passed=()):
    def body(*refs):
        source, out = refs[0], refs[1 + len(passed)]
        for n in range(copies):
            out[n] = source[...]

    anywhere = pl.BlockSpec(memory_space=pl.ANY)
    return pl.pallas_call(
        body,
        out_shape=[jax.ShapeDtypeStruct((copies, *block.shape), block.dtype)]
        + [jax.ShapeDtypeStruct(x.shape, x.dtype) for x in passed],
        in_specs=[VMEM] + [anywhere] * len(passed),
        out_specs=[VMEM] + [anywhere] * len(passed),
        input_output_aliases={1 + n: 1 + n for n in range(len(passed))},
        compiler_params=pltpu.CompilerParams(vmem_limit_bytes=8 << 20),
    )(block, *passed)


def after(*arrays):
    def body(*refs):
        pass

    anywhere = pl.BlockSpec(memory_space=pl.ANY)
    return pl.pallas_call(
        body,
        out_shape=[jax.ShapeDtypeStruct(x.shape, x.dtype) for x in arrays],
        in_specs=[anywhere] * len(arrays),
        out_specs=[anywhere] * len(arrays),
        input_output_aliases={n: n for n in range(len(arrays))},
        compiler_params=pltpu.CompilerParams(vmem_limit_bytes=1 << 20),
    )(*arrays)


def exchange(pieces, axes):
    return lax.all_to_all(pieces, axes, 0, 0, tiled=True)


def shards(state, cotangent, weights, lat_off, lon_off, basis, tap_val, tap_count):
    field, upstream = state[0], cotangent[0]
    rows, width, channels = field.shape
    kcount = weights.shape[0]
    wide = weights.reshape(-1, channels)
    tables = (lat_off.T, lon_off.T, basis.T, tap_val.T, tap_count)
    north, south = lat_blocks(field)
    strip = lax.ppermute(strip_for_west(field, north, south, upstream), "lon", lon_shift(-1))
    fields = (field, north, south, strip)
    cells = lax.axis_size(DP) * lax.axis_size(LAT) * rows * lax.axis_size("lon") * width
    nx, ny, nz = lax.axis_size(ALONG_X), lax.axis_size("y"), lax.axis_size("lon")
    made, dmixed, keep, send = forward(tables, wide, fields, upstream, 1.0 / math.sqrt(cells))
    piece = (keep.shape[0] // (nx * ny), channels)
    got = exchange(add_halves(keep, core_swap(send), nx), ALONG_X)
    part, dmixed = sum_pieces(got, jax.ShapeDtypeStruct((ny, *piece), BF16), (dmixed,))
    north, south = lat_blocks(dmixed)
    got = exchange(part, "y")
    (part,) = sum_pieces(got, jax.ShapeDtypeStruct((nz, *piece), F32))
    got = exchange(part, "lon")
    part, strip = sum_and_strip(got, ny, dmixed, north, south, made)
    strip = lax.ppermute(strip, "lon", lon_shift(1))
    got = exchange(part, "y")
    part, made = spread(got.reshape(-1, channels), nx, (made,))
    mine = exchange(part, ALONG_X).reshape(-1, channels)
    new_field, field_grad = backward(tables, wide, (dmixed, north, south, strip), made, upstream)
    mine, new_field, field_grad = after(mine, new_field, field_grad)
    weight_grad = join_halves(mine, core_swap(mine)).reshape(weights.shape)
    return new_field[None], field_grad[None], weight_grad


def solution(mesh):
    dp, lat, lon = (mesh.shape[name] for name in ("dp", "lat", "lon"))
    finer = jax.sharding.Mesh(mesh.devices.reshape(dp // 2, 2, lat // 2, 2, lon), DP + ("y", "x_lo", "lon"))
    cells = P(DP, LAT, "lon", None)
    return jax.shard_map(
        shards,
        mesh=finer,
        in_specs=(cells, cells, P(), P(), P(), P(), P(), P()),
        out_specs=(cells, cells, P()),
        check_vma=False,
    )
```

```python
import math

import jax
import jax.numpy as jnp
from jax import lax
from jax.experimental import pallas as pl
from jax.experimental.pallas import tpu as pltpu
from jax.sharding import PartitionSpec as P

H = 2
LONREACH = 24
RIM = 2 * LONREACH
LANES = 128
ROW = 192
EXT = ROW + RIM
SLOPE = math.sqrt(2.0 / math.pi)
CUBIC = 0.044715


SMEM = pl.BlockSpec(memory_space=pltpu.SMEM)
VMEM = pl.BlockSpec(memory_space=pltpu.VMEM)
BF16, F32 = jnp.bfloat16, jnp.float32
DP, LAT = ("x_hi", "core"), ("y", "x_lo")
ALONG_X = ("x_hi", "x_lo")


def forward_taps(tables, first, rows, kcount, pos, val):
    lat_off, lon_off, basis, tap_val, tap_count = tables
    taps = lat_off.shape[0]
    room = taps + 1
    for i in range(rows):
        row = first + i
        used = tap_count[row]
        counts = [jnp.int32(0) for _ in range(kcount)]
        for t in range(taps):
            where = (i + H + lat_off[t, row]) * EXT + LONREACH + lon_off[t, row]
            value = tap_val[t, row]
            kind = jnp.where(t < used, basis[t, row], kcount)
            for k in range(kcount):
                at = (i * kcount + k) * room + counts[k]
                pos[at] = where
                val[at] = value
                counts[k] = counts[k] + (kind == k).astype(jnp.int32)
        for k in range(kcount):
            pos[rows * kcount * room + i * kcount + k] = counts[k]


def backward_taps(tables, first, rows, pos, val):
    lat_off, lon_off, basis, tap_val, tap_count = tables
    taps, total = lat_off.shape
    high = rows + 2 * H
    room = high * taps + 1
    counts = [jnp.int32(0) for _ in range(rows)]
    for e in range(high):
        row = first + (e - H)
        inside = (row >= 0) & (row < total)
        row = jnp.clip(row, 0, total - 1)
        used = jnp.where(inside, tap_count[row], 0)
        for t in range(taps):
            where = (basis[t, row] * high + e) * EXT + LONREACH - lon_off[t, row]
            value = tap_val[t, row]
            target = jnp.where(t < used, e - H + lat_off[t, row], -1)
            for i in range(rows):
                at = i * room + counts[i]
                pos[at] = where
                val[at] = value
                counts[i] = counts[i] + (target == i).astype(jnp.int32)
    for i in range(rows):
        pos[rows * room + i] = counts[i]


def forward_kernel(lat_off, lon_off, basis, tap_val, tap_count, weights, own, north, south, east, ne, se, upstream,
                   new_state, dmixed, keep, send, pos, val, ext, up, z, dm, *, scale):
    rows, width, channels = own.shape
    kcount = weights.shape[0] // channels
    chunks = channels // LANES
    tables = (lat_off, lon_off, basis, tap_val, tap_count)
    room = lat_off.shape[0] + 1
    forward_taps(tables, lax.axis_index(LAT) * rows, rows, kcount, pos, val)
    for side, (mid, rim) in enumerate(((north, ne), (own, east), (south, se))):
        for r in range(rows):
            base = (side * rows + r) * EXT
            for c in range(chunks):
                lanes = slice(c * LANES, (c + 1) * LANES)
                ext[c, base : base + width, :] = mid[r, :, lanes].astype(F32)
                ext[c, base + width : base + width + RIM, :] = rim[r, :RIM, lanes].astype(F32)
                ext[c, base + width + RIM : base + EXT, :] = jnp.zeros((EXT - RIM - width, LANES), F32)
    for i in range(rows):
        kept = width - LONREACH
        up[i, :kept] = upstream[i].astype(F32)[LONREACH:]
        up[i, kept:width] = east[i].astype(F32)[RIM:]
    for i in range(rows):
        for k in range(kcount):
            for c in range(chunks):

                def add(n, acc):
                    at = (i * kcount + k) * room + n
                    return acc + val[at] * ext[c, pl.ds(pos[at], ROW), :]

                count = pos[rows * kcount * room + i * kcount + k]
                acc = lax.fori_loop(0, count, add, jnp.zeros((ROW, LANES), F32))
                col = k * channels + c * LANES
                z[i * ROW : (i + 1) * ROW, col : col + LANES] = acc.astype(BF16)
    mixed = jnp.dot(z[...], weights[...], preferred_element_type=F32)
    for i in range(rows):
        x = mixed[i * ROW : i * ROW + width]
        square = x * x
        t = jnp.tanh(SLOPE * (x + CUBIC * (square * x)))
        cdf = 0.5 * (1.0 + t)
        base = (H + i) * EXT + LONREACH
        field = jnp.concatenate([ext[c, base : base + width, :] for c in range(chunks)], axis=1)
        made = (field + x * cdf).astype(BF16)
        slope = cdf + x * (0.5 * (1.0 - t * t)) * (SLOPE * (1.0 + (3.0 * CUBIC) * square))
        d = (up[i, :width] * slope).astype(BF16)
        new_state[i] = made
        dmixed[i] = d
        dm[i * ROW : (i + 1) * ROW, :] = jnp.concatenate([d, jnp.zeros((ROW - width, channels), BF16)], axis=0)
    total = lax.dot_general(z[...], dm[...], (((0,), (0,)), ((), ())), preferred_element_type=F32)
    total = total * scale
    half = keep.shape[0]
    first = lax.axis_index("core") == 0
    keep[...] = jnp.where(first, total[:half], total[half:])
    send[...] = jnp.where(first, total[half:], total[:half]).astype(BF16)


def forward(tables, weights, fields, upstream, scale):
    rows, width, channels = upstream.shape
    wide = weights.shape[0]
    lists = rows * (wide // channels) * (tables[0].shape[0] + 1)
    block = jax.ShapeDtypeStruct((rows, width, channels), BF16)

    def body(*refs):
        forward_kernel(*refs, scale=scale)

    return pl.pallas_call(
        body,
        out_shape=[
            block,
            block,
            jax.ShapeDtypeStruct((wide // 2, channels), F32),
            jax.ShapeDtypeStruct((wide // 2, channels), BF16),
        ],
        in_specs=[SMEM] * 5 + [VMEM] * 8,
        out_specs=[VMEM] * 4,
        scratch_shapes=[
            pltpu.SMEM((lists + 64,), jnp.int32),
            pltpu.SMEM((lists,), F32),
            pltpu.VMEM((channels // LANES, (rows + 2 * H) * EXT, LANES), F32),
            pltpu.VMEM((rows, ROW, channels), F32),
            pltpu.VMEM((rows * ROW, wide), BF16),
            pltpu.VMEM((rows * ROW, channels), BF16),
        ],
        compiler_params=pltpu.CompilerParams(vmem_limit_bytes=24 << 20),
        cost_estimate=pl.CostEstimate(flops=2_000_000_000, bytes_accessed=8_000_000, transcendentals=140_000),
    )(*tables, weights, *fields, upstream)


def backward_kernel(lat_off, lon_off, basis, tap_val, tap_count, weights, own, north, south, strip, made, upstream,
                    new_state, state_grad, pos, val, dext, dz):
    rows, width, channels = own.shape
    kcount = weights.shape[0] // channels
    chunks = channels // LANES
    high = rows + 2 * H
    tables = (lat_off, lon_off, basis, tap_val, tap_count)
    room = high * lat_off.shape[0] + 1
    backward_taps(tables, lax.axis_index(LAT) * rows, rows, pos, val)
    for side, (mid, at) in enumerate(((north, 0), (own, 2 * RIM), (south, RIM))):
        for r in range(rows):
            base = (side * rows + r) * EXT
            dext[base : base + RIM, :] = strip[r, at : at + RIM]
            dext[base + RIM : base + EXT, :] = jnp.concatenate(
                [mid[r], jnp.zeros((EXT - RIM - width, channels), BF16)], axis=0
            )
    for i in range(rows):
        new_state[i] = jnp.concatenate([strip[i, 3 * RIM :], made[i, : width - LONREACH]], axis=0)
    for k in range(kcount):
        part = lax.dot_general(
            dext[...],
            weights[k * channels : (k + 1) * channels, :],
            (((1,), (1,)), ((), ())),
            preferred_element_type=F32,
        )
        part = part.astype(BF16).astype(F32)
        for c in range(chunks):
            dz[c, k * high * EXT : (k + 1) * high * EXT, :] = part[:, c * LANES : (c + 1) * LANES]
    for i in range(rows):
        for c in range(chunks):

            def add(n, acc):
                at = i * room + n
                return acc + val[at] * dz[c, pl.ds(pos[at], ROW), :]

            acc = lax.fori_loop(0, pos[rows * room + i], add, jnp.zeros((ROW, LANES), F32))
            lanes = slice(c * LANES, (c + 1) * LANES)
            adjoint = acc[:width].astype(BF16).astype(F32)
            state_grad[i, :, lanes] = (upstream[i, :, lanes].astype(F32) + adjoint).astype(BF16)


def backward(tables, weights, fields, made, upstream):
    rows, width, channels = upstream.shape
    high = rows + 2 * H
    kcount = weights.shape[0] // channels
    lists = rows * (high * tables[0].shape[0] + 1)
    block = jax.ShapeDtypeStruct((rows, width, channels), BF16)
    return pl.pallas_call(
        backward_kernel,
        out_shape=[block, block],
        in_specs=[SMEM] * 5 + [VMEM] * 7,
        out_specs=[VMEM] * 2,
        scratch_shapes=[
            pltpu.SMEM((lists + 8,), jnp.int32),
            pltpu.SMEM((lists,), F32),
            pltpu.VMEM((high * EXT, channels), BF16),
            pltpu.VMEM((channels // LANES, kcount * high * EXT, LANES), F32),
        ],
        compiler_params=pltpu.CompilerParams(vmem_limit_bytes=24 << 20),
        cost_estimate=pl.CostEstimate(flops=2_500_000_000, bytes_accessed=5_000_000, transcendentals=0),
    )(*tables, weights, *fields, made, upstream)


def lat_blocks(block):
    ends = lax.axis_size(LAT) - 1
    north = lax.ppermute(block, LAT, [(i, i + 1) for i in range(ends)])
    south = lax.ppermute(block, LAT, [(i + 1, i) for i in range(ends)])
    return north, south


def lon_shift(step):
    lons = lax.axis_size("lon")
    return [(j, (j + step) % lons) for j in range(lons)]


def lon_strips(side, rim):
    ends, lons = lax.axis_size(LAT) - 1, lax.axis_size("lon")
    along = lon_shift(-1)
    level = lax.ppermute(side, "lon", along)
    upper = lax.ppermute(rim, LAT + ("lon",), [(i * lons + c, (i + 1) * lons + d) for i in range(ends) for c, d in along])
    lower = lax.ppermute(rim, LAT + ("lon",), [((i + 1) * lons + c, i * lons + d) for i in range(ends) for c, d in along])
    return level, upper, lower


def core_swap(block):
    return lax.ppermute(block, "core", [(0, 1), (1, 0)])


def add_halves(keep, got, copies):
    def body(keep, got, out):
        rows = out.shape[1]
        total = (keep[...] + got[...].astype(F32)).astype(BF16)
        for n in range(copies):
            out[n] = total[n * rows : (n + 1) * rows]

    return pl.pallas_call(
        body,
        out_shape=jax.ShapeDtypeStruct((copies, keep.shape[0] // copies, keep.shape[1]), BF16),
        in_specs=[VMEM] * 2,
        out_specs=VMEM,
        compiler_params=pltpu.CompilerParams(vmem_limit_bytes=12 << 20),
    )(keep, got)


def join_halves(mine, other):
    def body(mine, other, out):
        half = mine.shape[0]
        first = lax.axis_index("core") == 0
        out[:half] = jnp.where(first, mine[...], other[...])
        out[half:] = jnp.where(first, other[...], mine[...])

    return pl.pallas_call(
        body,
        out_shape=jax.ShapeDtypeStruct((2 * mine.shape[0], mine.shape[1]), BF16),
        in_specs=[VMEM] * 2,
        out_specs=VMEM,
        compiler_params=pltpu.CompilerParams(vmem_limit_bytes=12 << 20),
    )(mine, other)


def sum_and_strip(pieces, copies, dmixed, north, south, made):
    def body(part, dmixed, north, south, made, out, strip):
        total = part[0]
        for n in range(1, part.shape[0]):
            total = total + part[n]
        total = total.astype(out.dtype)
        for n in range(copies):
            out[n] = total
        rows, width, _ = dmixed.shape
        for r in range(rows):
            for n, source in enumerate((north, south, dmixed)):
                strip[r, n * RIM : (n + 1) * RIM] = source[r, width - RIM :]
            strip[r, 3 * RIM :] = made[r, width - LONREACH :]

    rows, _, channels = dmixed.shape
    return pl.pallas_call(
        body,
        out_shape=[
            jax.ShapeDtypeStruct((copies, *pieces.shape[1:]), BF16),
            jax.ShapeDtypeStruct((rows, 3 * RIM + LONREACH, channels), BF16),
        ],
        in_specs=[VMEM] * 5,
        out_specs=[VMEM] * 2,
        compiler_params=pltpu.CompilerParams(vmem_limit_bytes=12 << 20),
    )(pieces, dmixed, north, south, made)


def sum_pieces(pieces, out_shape, passed=()):
    def body(*refs):
        part, out = refs[0], refs[1 + len(passed)]
        total = part[0].astype(F32)
        for n in range(1, part.shape[0]):
            total = total + part[n].astype(F32)
        total = total.astype(out.dtype)
        rows = out.shape[1]
        for n in range(out.shape[0]):
            out[n] = total if rows == total.shape[0] else total[n * rows : (n + 1) * rows]

    anywhere = pl.BlockSpec(memory_space=pl.ANY)
    return pl.pallas_call(
        body,
        out_shape=[out_shape] + [jax.ShapeDtypeStruct(x.shape, x.dtype) for x in passed],
        in_specs=[VMEM] + [anywhere] * len(passed),
        out_specs=[VMEM] + [anywhere] * len(passed),
        input_output_aliases={1 + n: 1 + n for n in range(len(passed))},
        compiler_params=pltpu.CompilerParams(vmem_limit_bytes=8 << 20),
    )(pieces, *passed)


def spread(block, copies, passed=()):
    def body(*refs):
        source, out = refs[0], refs[1 + len(passed)]
        for n in range(copies):
            out[n] = source[...]

    anywhere = pl.BlockSpec(memory_space=pl.ANY)
    return pl.pallas_call(
        body,
        out_shape=[jax.ShapeDtypeStruct((copies, *block.shape), block.dtype)]
        + [jax.ShapeDtypeStruct(x.shape, x.dtype) for x in passed],
        in_specs=[VMEM] + [anywhere] * len(passed),
        out_specs=[VMEM] + [anywhere] * len(passed),
        input_output_aliases={1 + n: 1 + n for n in range(len(passed))},
        compiler_params=pltpu.CompilerParams(vmem_limit_bytes=8 << 20),
    )(block, *passed)


def after(*arrays):
    def body(*refs):
        pass

    anywhere = pl.BlockSpec(memory_space=pl.ANY)
    return pl.pallas_call(
        body,
        out_shape=[jax.ShapeDtypeStruct(x.shape, x.dtype) for x in arrays],
        in_specs=[anywhere] * len(arrays),
        out_specs=[anywhere] * len(arrays),
        input_output_aliases={n: n for n in range(len(arrays))},
        compiler_params=pltpu.CompilerParams(vmem_limit_bytes=1 << 20),
    )(*arrays)


def exchange(pieces, axes):
    return lax.all_to_all(pieces, axes, 0, 0, tiled=True)


def shards(state, cotangent, weights, lat_off, lon_off, basis, tap_val, tap_count):
    field, upstream = state[0], cotangent[0]
    rows, width, channels = field.shape
    kcount = weights.shape[0]
    wide = weights.reshape(-1, channels)
    tables = (lat_off.T, lon_off.T, basis.T, tap_val.T, tap_count)
    side = jnp.concatenate([field[:, :RIM], upstream[:, :LONREACH]], axis=1)
    fields = (field, *lat_blocks(field), *lon_strips(side, field[:, :RIM]))
    cells = lax.axis_size(DP) * lax.axis_size(LAT) * rows * lax.axis_size("lon") * width
    nx, ny, nz = lax.axis_size(ALONG_X), lax.axis_size("y"), lax.axis_size("lon")
    made, dmixed, keep, send = forward(tables, wide, fields, upstream, 1.0 / math.sqrt(cells))
    piece = (keep.shape[0] // (nx * ny), channels)
    got = exchange(add_halves(keep, core_swap(send), nx), ALONG_X)
    part, dmixed = sum_pieces(got, jax.ShapeDtypeStruct((ny, *piece), BF16), (dmixed,))
    north, south = lat_blocks(dmixed)
    got = exchange(part, "y")
    (part,) = sum_pieces(got, jax.ShapeDtypeStruct((nz, *piece), F32))
    got = exchange(part, "lon")
    part, strip = sum_and_strip(got, ny, dmixed, north, south, made)
    strip = lax.ppermute(strip, "lon", lon_shift(1))
    got = exchange(part, "y")
    part, made = spread(got.reshape(-1, channels), nx, (made,))
    mine = exchange(part, ALONG_X).reshape(-1, channels)
    new_field, field_grad = backward(tables, wide, (dmixed, north, south, strip), made, upstream)
    mine, new_field, field_grad = after(mine, new_field, field_grad)
    weight_grad = join_halves(mine, core_swap(mine)).reshape(weights.shape)
    return new_field[None], field_grad[None], weight_grad


def solution(mesh):
    dp, lat, lon = (mesh.shape[name] for name in ("dp", "lat", "lon"))
    finer = jax.sharding.Mesh(mesh.devices.reshape(dp // 2, 2, lat // 2, 2, lon), DP + ("y", "x_lo", "lon"))
    cells = P(DP, LAT, "lon", None)
    return jax.shard_map(
        shards,
        mesh=finer,
        in_specs=(cells, cells, P(), P(), P(), P(), P(), P()),
        out_specs=(cells, cells, P()),
        check_vma=False,
    )
```
